32 devices in a mesh: layer: 4 (over y, x), tok: 8 (over z, core).
Axes of the slice: x: 2, y: 2, z: 4, core: 2. Of those that a mesh axis runs over, the one named last changes fastest.
Arguments:
- layer_inputs: bfloat16 [4, 256, 2048], P('layer', 'tok'), may hold values from -6 to 6
- layer_targets: bfloat16 [4, 256, 2048], P('layer', 'tok'), may hold values from -12 to 12
- row_order: int32 [256], replicated, may hold values from 0 to 255, each once
- encoder_weight: bfloat16 [4, 2048, 4096], P('layer', None, 'tok'), may hold values from -0.125 to 0.125
- encoder_bias: float32 [4, 4096], P('layer', 'tok'), may hold values from -3 to 3
- decoder_weight: bfloat16 [4, 4, 4096, 2048], P('layer', None, 'tok'), may hold values from -1 to 1
- decoder_bias: float32 [4, 2048], P('layer'), may hold values from -0.6 to 0.6
Outputs:
- encoder_grad: bfloat16 [4, 2048, 4096], P('layer', None, 'tok')
- feature_grad: float32 [4, 4096], P('layer', 'tok')
- decoder_grad: bfloat16 [4, 4, 4096, 2048], P('layer', None, 'tok')
- output_grad: float32 [4, 2048], P('layer')
The draws below stay inside these ranges and needn't reach their ends.
Inputs may be any that keep to these rules, and one draw needn't show every extreme that they name: Row i of layer_targets belongs to the token in row row_order[i] of layer_inputs, in every layer; each row index appears once.
All inputs are finite; a program needn't handle non-finite values.
Results may differ from the reference program's by a relative error of at most 0.015.
Values may be sent and summed in bfloat16 or wider, within the bound.
No kernel may reach another device: no remote copies, remote signals or barrier semaphores. Data moves between devices by JAX's collectives and lax.ppermute only.
A program may use at most 128 MiB of HBM per device.

```python
import math
import jax
import jax.numpy as jnp
from jax import lax

D = 2048
FC = 4096
L = 4
TOKENS = 256


def draw_decoder_weight(key, part):
    subkeys = jax.random.split(key, 3)
    shape = (L, L, FC, D)
    base_noise = jnp.clip(jax.random.normal(subkeys[0], shape, jnp.float32), -4.0, 4.0)
    growth = 3.0
    row_scale = jnp.exp(jax.random.uniform(subkeys[1], (L, L, FC, 1), jnp.float32, -1.1513, 1.1513))
    col_scale = jnp.exp(jax.random.uniform(subkeys[2], (L, 1, 1, D), jnp.float32, -1.1513, 1.1513))
    layer_index = jnp.arange(L).astype(jnp.float32)
    layer_scale = growth ** (layer_index / max(L - 1, 1)) / jnp.sqrt(FC * (layer_index + 1.0))
    values = base_noise * row_scale * col_scale * layer_scale.reshape(L, 1, 1, 1)
    return jnp.clip(values, -1.0, 1.0).astype(jnp.bfloat16)


def level_of(stream_key, extent, cuts, low, top_value):
    factor_of = 1.0
    for position, blocks in cuts:
        steps = jax.random.uniform(jax.random.fold_in(jax.random.fold_in(stream_key, 6), position), (blocks,), jnp.float32, low / len(cuts), top_value / len(cuts))
        factor_of = factor_of * jnp.repeat(jnp.exp(steps), extent[position] // blocks).reshape((-1,) + (1,) * (len(extent) - 1 - position))
    return factor_of


def scatter_about(stream_key, dims, scale, bound, pieces=(), held_as=jnp.bfloat16):
    result = jax.random.normal(stream_key, dims, jnp.float32) * scale
    if len(pieces) > 0:
        result = level_of(stream_key, dims, pieces, -0.22, 0.18) * result
    return jnp.clip(result, min=-bound, max=bound).astype(held_as)


def setup_inputs(seed: int = 0) -> dict:
    key_list = jax.random.split(jax.random.key(seed), 8)
    return {
        "layer_inputs": scatter_about(key_list[0], (L, TOKENS, D), 1.0, 6.0, ((0, 4), (1, 8))),
        "layer_targets": scatter_about(key_list[1], (L, TOKENS, D), 2.0, 12.0, ((0, 4), (1, 8))),
        "row_order": jax.random.permutation(key_list[2], TOKENS).astype(jnp.int32),
        "encoder_weight": scatter_about(key_list[3], (L, D, FC), D ** -0.5, 0.125, ((0, 4), (2, 8))),
        "encoder_bias": scatter_about(key_list[4], (L, FC), 0.5, 3.0, ((0, 4), (1, 8)), jnp.float32),
        "decoder_weight": draw_decoder_weight(jax.random.fold_in(key_list[7], 71), 0),
        "decoder_bias": scatter_about(key_list[6], (L, D), 0.1, 0.6, ((0, 4),), jnp.float32),
    }


def reference(layer_inputs, layer_targets, row_order, encoder_weight, encoder_bias, decoder_weight, decoder_bias):
    layers = layer_inputs.shape[0]
    row_total = layer_inputs.shape[1]
    width = layer_inputs.shape[2]
    features = encoder_weight.shape[2]
    loss_scale = 1.0 / math.sqrt(row_total)
    contract_rows = (((0,), (0,)), ((), ()))
    contract_cols = (((1,), (1,)), ((), ()))
    ordered_list = []
    pre_list = []
    act_list = []
    norm_list = []
    for source in range(layers):
        ordered = jnp.take(layer_inputs[source], row_order.astype(jnp.int32), axis=0)
        pre_act = jnp.dot(ordered, encoder_weight[source], preferred_element_type=jnp.float32) + encoder_bias[source]
        ordered_list.append(ordered)
        pre_list.append(pre_act)
        act_list.append(jnp.maximum(pre_act, 0.0).astype(jnp.bfloat16))
        squares = jnp.zeros((features,), jnp.float32)
        for target in range(source, layers):
            squares = squares + lax.optimization_barrier(jnp.sum(jnp.square(decoder_weight[target, source].astype(jnp.float32)), axis=1))
        norm_list.append(jnp.sqrt(squares + 1e-06))
    resid_list = []
    output_rows = []
    for target in range(layers):
        decoded = jnp.zeros((row_total, width), jnp.float32)
        for source in range(target + 1):
            decoded = decoded + jnp.dot(act_list[source], decoder_weight[target, source], preferred_element_type=jnp.float32)
        resid_full = (decoded + decoder_bias[target] - layer_targets[target].astype(jnp.float32)) * loss_scale
        output_rows.append(lax.optimization_barrier(jnp.sum(resid_full, axis=0)))
        resid_list.append(resid_full.astype(jnp.bfloat16))
    encoder_rows = []
    feature_rows = []
    decoder_rows = []
    for source in range(layers):
        grad_acts = jnp.zeros((row_total, features), jnp.float32)
        for target in range(source, layers):
            grad_acts = grad_acts + lax.dot_general(resid_list[target], decoder_weight[target, source], contract_cols, preferred_element_type=jnp.float32)
        grad_pre = jnp.where(pre_list[source] > 0, grad_acts + norm_list[source] * loss_scale, 0.0)
        grad_low = grad_pre.astype(jnp.bfloat16)
        encoder_rows.append(lax.dot_general(ordered_list[source], grad_low, contract_rows, preferred_element_type=jnp.float32).astype(jnp.bfloat16))
        feature_rows.append(lax.optimization_barrier(jnp.sum(grad_pre, axis=0)))
    for target in range(layers):
        blocks = []
        for source in range(layers):
            if source <= target:
                act_sums = lax.optimization_barrier(jnp.sum(act_list[source].astype(jnp.float32), axis=0))
                factor = act_sums * loss_scale / norm_list[source]
                product = lax.dot_general(act_list[source], resid_list[target], contract_rows, preferred_element_type=jnp.float32)
                blocks.append((product + factor[:, None] * decoder_weight[target, source].astype(jnp.float32)).astype(jnp.bfloat16))
            else:
                blocks.append(jnp.zeros((features, width), jnp.bfloat16))
        decoder_rows.append(jnp.stack(blocks))
    return (jnp.stack(encoder_rows), jnp.stack(feature_rows), jnp.stack(decoder_rows), jnp.stack(output_rows))
```

```python
import functools
import math

import jax
import jax.numpy as jnp
from jax import lax
from jax.experimental import pallas as pl
from jax.experimental.pallas import tpu as pltpu
from jax.sharding import PartitionSpec as P

BF16 = jnp.bfloat16
F32 = jnp.float32
VMEM_LIMIT = 48 * 1024 * 1024


def whole(count):
    return [pl.BlockSpec(memory_space=pltpu.VMEM)] * count


def call(kernel, out_shape, in_specs, out_specs, scratch, flops, moved):
    return pl.pallas_call(
        kernel,
        out_shape=out_shape,
        in_specs=in_specs,
        out_specs=out_specs,
        scratch_shapes=scratch,
        compiler_params=pltpu.CompilerParams(vmem_limit_bytes=VMEM_LIMIT),
        cost_estimate=pl.CostEstimate(flops=flops, bytes_accessed=moved, transcendentals=0),
    )


def encode_kernel(count, *refs):
    pieces, (weight, bias, out, rows) = refs[:count], refs[count:]
    height = pieces[0].shape[0]
    for index, piece in enumerate(pieces):
        rows[pl.ds(index * height, height), :] = piece[...]
    value = jnp.dot(rows[...], weight[...], preferred_element_type=F32) + bias[...]
    out[...] = jnp.maximum(value, 0.0).astype(BF16)


def decode_kernel(layers, pieces, columns, target_ref, order_ref, *refs):
    acts = refs[: 2 * layers]
    weights, order_out, keep, send, buffer, sems = refs[2 * layers :]
    target = target_ref[0]
    features = acts[0].shape[1]
    half = acts[0].shape[0]
    width = weights.shape[2]
    copies = []
    for part in range(width // columns):
        copy = pltpu.make_async_copy(
            weights.at[:, :, pl.ds(part * columns, columns)],
            buffer.at[:, :, pl.ds(part * columns, columns)],
            sems.at[part],
        )
        copy.start()
        copies.append(copy)
    order = order_ref[...]
    for offset in range(layers):
        source = target ^ offset
        place = pl.ds(pl.multiple_of(source * features, features), features)
        low = jnp.dot(order[:, :half], acts[2 * offset][...], preferred_element_type=F32)
        high = jnp.dot(order[:, half:], acts[2 * offset + 1][...], preferred_element_type=F32)
        used = jnp.where(source <= target, 1.0, 0.0)
        order_out[:, place] = ((low + high) * used).astype(BF16)
    quarter = half // 2
    for part, copy in enumerate(copies):
        copy.wait()
        lanes = pl.ds(part * columns, columns)
        block = buffer[:, :, lanes].reshape(layers * features, columns)
        value = jnp.dot(order_out[...], block, preferred_element_type=F32).astype(BF16)
        keep[pl.ds(0, quarter), lanes] = value[:quarter]
        send[pl.ds(0, quarter), lanes] = value[quarter : 2 * quarter]
        keep[pl.ds(quarter, quarter), lanes] = value[2 * quarter : 3 * quarter]
        send[pl.ds(quarter, quarter), lanes] = value[3 * quarter :]


def grad_kernel(layers, count, target_ref, *refs):
    pieces = refs[:count]
    weights = refs[count]
    outs = refs[count + 1 : count + 1 + layers]
    rows, buffer, sems = refs[count + 1 + layers :]
    target = target_ref[0]
    sequence = list(range(1, layers)) + [0]
    copies = {}
    for offset in sequence:
        copy = pltpu.make_async_copy(
            weights.at[target ^ offset], buffer.at[offset], sems.at[offset]
        )
        copy.start()
        copies[offset] = copy
    height = pieces[0].shape[0]
    for index, piece in enumerate(pieces):
        rows[pl.ds(index * height, height), :] = piece[...]
    for offset in sequence:
        copies[offset].wait()
        value = lax.dot_general(
            rows[...], buffer[offset], (((1,), (1,)), ((), ())), preferred_element_type=F32
        )
        used = (target ^ offset) <= target
        outs[offset][...] = jnp.where(used, value, 0.0).astype(outs[offset].dtype)


def decoder_grad_kernel(count, loss_scale, target_ref, acts, norms, *refs):
    pieces = refs[:count]
    weights, out, rows = refs[count:]
    source = pl.program_id(0)
    height = pieces[0].shape[0]

    @pl.when(jnp.logical_and(source == 0, pl.program_id(1) == 0))
    def _():
        for index, piece in enumerate(pieces):
            rows[pl.ds(index * height, height), :] = piece[...]

    @pl.when(source <= target_ref[0])
    def _():
        columns = out.shape[2]
        lanes = pl.ds(pl.multiple_of(pl.program_id(1) * columns, columns), columns)
        block = acts[...]
        product = lax.dot_general(
            block, rows[:, lanes], (((0,), (0,)), ((), ())), preferred_element_type=F32
        )
        ones = jnp.ones((block.shape[0], 128), BF16)
        sums = lax.dot_general(block, ones, (((0,), (0,)), ((), ())), preferred_element_type=F32)
        norm = jnp.broadcast_to(norms[0], (128, norms.shape[2])).T
        factor = sums * loss_scale / norm
        for part in range(columns // 128):
            cut = slice(part * 128, part * 128 + 128)
            out[0, :, cut] = (
                product[:, cut] + factor * weights[0, :, cut].astype(F32)
            ).astype(BF16)

    @pl.when(source > target_ref[0])
    def _():
        out[...] = jnp.zeros(out.shape, out.dtype)


def on_device(
    layer_inputs,
    layer_targets,
    row_order,
    encoder_weight,
    encoder_bias,
    decoder_weight,
    decoder_bias,
):
    layers = lax.axis_size("layer")
    ranks = lax.axis_size("tok")
    lines = ranks // 2
    row_total = row_order.shape[0]
    height = row_total // ranks
    loss_scale = 1.0 / math.sqrt(row_total)
    target = lax.axis_index("layer")
    rank = lax.axis_index("tok")
    target_id = target.astype(jnp.int32).reshape(1)
    weights = decoder_weight[0]
    features, width = weights.shape[1:]
    half = row_total // 2

    def swap_tok(value, step):
        return lax.ppermute(value, "tok", [(i, i ^ step) for i in range(ranks)])

    def swap_layer(value, step):
        return lax.ppermute(value, "layer", [(i, i ^ step) for i in range(layers)])

    def gather_lines(own):
        lane = {0: own}
        for line in sorted(range(1, lines), key=lambda j: (bin(j).count("1"), j)):
            low = line & -line
            lane[line] = swap_tok(lane[line ^ low], 2 * low)
        other = {line: swap_tok(lane[line], 1) for line in range(lines)}
        first, last = range(lines // 2), range(lines // 2, lines)
        return [
            [lane[j] for j in group] + [other[j] for j in group] for group in (first, last)
        ]

    relative = []
    for group in (range(lines // 2), range(lines // 2, lines)):
        for core in range(2):
            relative += [2 * j + core for j in group]
    ordered_ranks = row_order.reshape(ranks, height)
    wanted = jnp.concatenate(
        [lax.dynamic_index_in_dim(ordered_ranks, rank ^ j, 0, keepdims=False) for j in relative]
    )
    held = (
        (rank ^ jnp.array(relative, jnp.int32))[:, None] * height
        + jnp.arange(height, dtype=jnp.int32)[None, :]
    ).reshape(row_total)
    order = (wanted[:, None] == held[None, :]).astype(BF16)

    inputs = gather_lines(layer_inputs[0])
    acts = []
    for pieces in inputs:
        own = call(
            functools.partial(encode_kernel, len(pieces)),
            jax.ShapeDtypeStruct((half, features), BF16),
            whole(len(pieces) + 2),
            pl.BlockSpec(memory_space=pltpu.VMEM),
            [pltpu.VMEM((half, width), BF16)],
            2 * half * width * features,
            2 * width * features,
        )(*pieces, encoder_weight[0], encoder_bias)
        acts.append([own] + [swap_layer(own, step) for step in range(1, layers)])

    squares = jnp.sum(jnp.square(weights.astype(F32)), axis=2)
    active = (jnp.arange(layers) <= target)[:, None]
    squares = jnp.where(active, squares, 0.0)
    norm_sq = squares
    for step in range(1, layers):
        norm_sq = norm_sq + swap_layer(squares, step)
    norms = jnp.sqrt(norm_sq + 1e-06)

    columns = min(512, width)
    any_space = pl.BlockSpec(memory_space=pl.ANY)
    scalar = pl.BlockSpec(memory_space=pltpu.SMEM)
    flat_acts = [acts[part][step] for step in range(layers) for part in range(2)]
    acts_all, keep, send = call(
        functools.partial(decode_kernel, layers, lines, columns),
        (
            jax.ShapeDtypeStruct((row_total, layers * features), BF16),
            jax.ShapeDtypeStruct((half, width), BF16),
            jax.ShapeDtypeStruct((half, width), BF16),
        ),
        [scalar] + whole(1 + 2 * layers) + [any_space],
        tuple(whole(3)),
        [
            pltpu.VMEM((layers, features, width), BF16),
            pltpu.SemaphoreType.DMA((width // columns,)),
        ],
        2 * row_total * layers * features * width,
        2 * layers * features * width,
    )(target_id, order, *flat_acts, weights)

    received = swap_tok(send, 1).astype(F32).reshape(lines, height, width)
    kept = keep.astype(F32).reshape(lines, height, width)
    parts = {j: kept[j] + received[j] for j in range(lines)}
    after = None
    for line in reversed(range(1, lines)):
        low = line & -line
        block = parts[line].astype(BF16)
        if after is not None:
            block, after = lax.optimization_barrier((block, after))
        after = swap_tok(block, 2 * low)
        parts[line ^ low] = parts[line ^ low] + after.astype(F32)
    resid_full = (
        parts[0] + decoder_bias[0] - layer_targets[0].astype(F32)
    ) * loss_scale
    resid = gather_lines(resid_full.astype(BF16))

    own_acts = [acts_all_part for acts_all_part in (acts_all[:half], acts_all[half:])]
    grads = []
    for pieces in resid:
        outs = call(
            functools.partial(grad_kernel, layers, len(pieces)),
            tuple(
                jax.ShapeDtypeStruct((half, features), BF16 if step else F32)
                for step in range(layers)
            ),
            [scalar] + whole(len(pieces)) + [any_space],
            tuple(whole(layers)),
            [
                pltpu.VMEM((half, width), BF16),
                pltpu.VMEM((layers, features, width), BF16),
                pltpu.SemaphoreType.DMA((layers,)),
            ],
            2 * half * layers * features * width,
            2 * layers * features * width,
        )(target_id, *pieces, weights)
        total = outs[0]
        for step in range(1, layers):
            total = total + swap_layer(outs[step], step).astype(F32)
        grads.append(total)

    all_pieces = resid[0] + resid[1]
    cut = min(1024, width)
    decoder_grad = pl.pallas_call(
        functools.partial(decoder_grad_kernel, len(all_pieces), loss_scale),
        out_shape=jax.ShapeDtypeStruct((layers, features, width), BF16),
        grid=(layers, width // cut),
        in_specs=[
            scalar,
            pl.BlockSpec((row_total, features), lambda s, n: (0, s)),
            pl.BlockSpec((1, 1, features), lambda s, n: (s, 0, 0)),
            *[pl.BlockSpec((height, width), lambda s, n: (0, 0)) for _ in all_pieces],
            pl.BlockSpec((1, features, cut), lambda s, n: (s, 0, n)),
        ],
        out_specs=pl.BlockSpec((1, features, cut), lambda s, n: (s, 0, n)),
        scratch_shapes=[pltpu.VMEM((row_total, width), BF16)],
        compiler_params=pltpu.CompilerParams(
            vmem_limit_bytes=VMEM_LIMIT, dimension_semantics=("arbitrary", "arbitrary")
        ),
        cost_estimate=pl.CostEstimate(
            flops=2 * row_total * layers * features * width,
            bytes_accessed=4 * layers * features * width,
            transcendentals=0,
        ),
    )(target_id, acts_all, norms[:, None, :], *all_pieces, weights)
    bias_grad = sum(jnp.sum(piece.astype(F32), axis=0) for piece in all_pieces)

    own_norm = lax.dynamic_index_in_dim(norms, target, 0, keepdims=False)
    ordered = lax.dot_general(
        jnp.concatenate(inputs[0] + inputs[1]),
        order,
        (((0,), (1,)), ((), ())),
        preferred_element_type=F32,
    ).astype(BF16)
    own_all = lax.dynamic_slice_in_dim(acts_all, target * features, features, axis=1)
    grad_pre = jnp.where(
        own_all > 0, jnp.concatenate(grads) + own_norm * loss_scale, 0.0
    )
    encoder_grad = jnp.dot(
        ordered, grad_pre.astype(BF16), preferred_element_type=F32
    ).astype(BF16)
    feature_grad = jnp.sum(grad_pre, axis=0)
    return (encoder_grad[None], feature_grad[None], decoder_grad[None], bias_grad[None])


def solution(mesh):
    placed = (
        P("layer", "tok", None),
        P("layer", "tok", None),
        P(),
        P("layer", None, "tok"),
        P("layer", "tok"),
        P("layer", None, "tok", None),
        P("layer", None),
    )
    return jax.shard_map(
        on_device,
        mesh=mesh,
        in_specs=placed,
        out_specs=(
            P("layer", None, "tok"),
            P("layer", "tok"),
            P("layer", None, "tok", None),
            P("layer", None),
        ),
        check_vma=False,
    )
```

```python
import functools
import math

import jax
import jax.numpy as jnp
from jax import lax
from jax.experimental import pallas as pl
from jax.experimental.pallas import tpu as pltpu
from jax.sharding import PartitionSpec as P

BF16 = jnp.bfloat16
F32 = jnp.float32
VMEM_LIMIT = 16 * 1024 * 1024
MICROSECOND = 1_150_000_000


def whole(count):
    return [pl.BlockSpec(memory_space=pltpu.VMEM)] * count


def call(kernel, out_shape, in_specs, out_specs, scratch, flops, moved, limit=VMEM_LIMIT):
    return pl.pallas_call(
        kernel,
        out_shape=out_shape,
        in_specs=in_specs,
        out_specs=out_specs,
        scratch_shapes=scratch,
        compiler_params=pltpu.CompilerParams(vmem_limit_bytes=limit),
        cost_estimate=pl.CostEstimate(flops=flops, bytes_accessed=moved, transcendentals=0),
    )


def table_kernel(relative, rows_ref, order, table):
    rank = lax.axis_index("tok")
    total_rows = table.shape[0]
    height = total_rows // len(relative)
    lane = lax.broadcasted_iota(jnp.int32, (1, total_rows), 1)
    held_rows = lane % height
    for index, offset in enumerate(relative):
        held_rows = held_rows + jnp.where(lane // height == index, (rank ^ offset) * height, 0)
    wanted = jnp.broadcast_to(rows_ref[...], (total_rows, total_rows)).T
    table[...] = jnp.where(wanted == held_rows, 1.0, 0.0)
    for index, offset in enumerate(relative):
        start = pl.multiple_of((rank ^ offset) * height, height)
        order[pl.ds(index * height, height), :] = table[pl.ds(start, height), :].astype(BF16)


def norm_kernel(weights, squares):
    layers, features, width = weights.shape
    target = lax.axis_index("layer")
    for source in range(layers):
        total = jnp.zeros((features, 128), F32)
        for part in range(width // 128):
            value = weights[source, :, pl.ds(part * 128, 128)].astype(F32)
            total = total + value * value
        column = jnp.sum(total, axis=1, keepdims=True)
        row = jnp.broadcast_to(column, (features, 128)).T[:1]
        squares[pl.ds(source, 1), :] = jnp.where(source <= target, row, 0.0)


def gather_rows(pieces, rows):
    height = pieces[0].shape[0]
    for index, piece in enumerate(pieces):
        rows[pl.ds(index * height, height), :] = piece[...]


def gather_parts(parts, rows):
    start = 0
    for part in parts:
        rows[pl.ds(start, part.shape[0]), :] = part[...]
        start += part.shape[0]


def encode_kernel(count, *refs):
    pieces, (weight, bias, out, rows) = refs[:count], refs[count:]
    gather_rows(pieces, rows)
    value = jnp.dot(rows[...], weight[...], preferred_element_type=F32) + bias[...]
    out[...] = jnp.maximum(value, 0.0).astype(BF16)


def encode_last_kernel(count, *refs):
    pieces, (weight, bias, squares, out, rows, extra) = refs[:count], refs[count:]
    gather_rows(pieces, rows)
    value = jnp.dot(rows[...], weight[...], preferred_element_type=F32) + bias[...]
    out[pl.ds(0, rows.shape[0]), :] = jnp.maximum(value, 0.0).astype(BF16)
    extra[...] = jnp.zeros(extra.shape, F32)
    rest = squares[...]
    layers = rest.shape[0]
    for part in range(3):
        term = rest.astype(BF16).astype(F32)
        extra[pl.ds(part * layers, layers), :] = term
        rest = rest - term
    out[pl.ds(rows.shape[0], extra.shape[0]), :] = extra[...].astype(BF16)


def sort_kernel(layers, order, *refs):
    acts, out = refs[:layers], refs[layers]
    target = lax.axis_index("layer")
    first, features = acts[0].shape
    for offset in range(layers):
        place = pl.ds(pl.multiple_of((target ^ offset) * features, features), features)
        out[:, place] = jnp.dot(order[:, :first], acts[offset][...], preferred_element_type=F32)


def decode_kernel(layers, last, columns, order_ref, first_sorted, *refs):
    acts, weights = refs[:layers], refs[layers]
    acts_out, keep, send, norms = refs[layers + 1 :]
    target = lax.axis_index("layer")
    features, width = weights.shape[1:]
    total_rows = order_ref.shape[0]
    first = total_rows - last
    for offset in range(layers):
        source = target ^ offset
        place = pl.ds(pl.multiple_of(source * features, features), features)
        value = jnp.dot(
            order_ref[:, pl.ds(first, last)],
            acts[offset][pl.ds(0, last), :],
            preferred_element_type=F32,
        )
        used = jnp.where(source <= target, 1.0, 0.0)
        acts_out[:, place] = ((first_sorted[:, place] + value) * used).astype(BF16)
    near, far = first // 2, last // 2
    for part in range(width // columns):
        lanes = pl.ds(part * columns, columns)
        block = weights[:, :, lanes].reshape(layers * features, columns)
        value = jnp.dot(acts_out[...], block, preferred_element_type=F32).astype(BF16)
        keep[pl.ds(0, near), lanes] = value[:near]
        send[pl.ds(0, near), lanes] = value[near:first]
        keep[pl.ds(near, far), lanes] = value[first : first + far]
        send[pl.ds(near, far), lanes] = value[first + far :]
    total = jnp.zeros((layers, features), F32)
    for offset in range(layers):
        value = acts[offset][pl.ds(last, acts[0].shape[0] - last), :].astype(F32)
        for part in range(3):
            total = total + value[part * layers : (part + 1) * layers]
    norms[...] = jnp.sqrt(total + 1e-06)


def order_kernel(count, *refs):
    pieces, (order, out, rows) = refs[:count], refs[count:]
    gather_rows(pieces, rows)
    out[...] = lax.dot_general(
        rows[...], order[...], (((0,), (1,)), ((), ())), preferred_element_type=F32
    ).astype(BF16)


def grad_kernel(layers, count, *refs):
    pieces, weights = refs[:count], refs[count]
    outs, rows = refs[count + 1 : count + 1 + layers], refs[count + 1 + layers]
    target = lax.axis_index("layer")
    gather_rows(pieces, rows)
    for offset in range(layers):
        source = target ^ offset
        value = lax.dot_general(
            rows[...], weights[source], (((1,), (1,)), ((), ())), preferred_element_type=F32
        )
        outs[offset][...] = jnp.where(source <= target, value, 0.0).astype(outs[offset].dtype)


def decoder_grad_kernel(loss_scale, acts, norms, main_rows, last_rows, weights, *refs):
    out, bias_out, rows, slots, sems = refs
    layers, features, width = weights.shape
    depth, tall = slots.shape[:2]
    steps = features // tall
    pending = [None] * depth
    gather_parts((main_rows, last_rows), rows)
    bias_out[...] = jnp.sum(rows[...].astype(F32), axis=0, keepdims=True)
    for source in range(layers):
        used = source <= lax.axis_index("layer")
        for step in range(steps):
            slot = (source * steps + step) % depth
            if pending[slot] is not None:
                pending[slot].wait()
            block = acts[:, pl.ds(source * features + step * tall, tall)]
            sums = jnp.sum(block.astype(F32), axis=0, keepdims=True)
            norm = norms[pl.ds(source, 1), pl.ds(step * tall, tall)]
            factor_row = jnp.where(used, sums * loss_scale / norm, 0.0)
            factor = jnp.broadcast_to(factor_row, (128, tall)).T
            product = lax.dot_general(
                block, rows[...], (((0,), (0,)), ((), ())), preferred_element_type=F32
            )
            for part in range(width // 128):
                cut = slice(part * 128, part * 128 + 128)
                value = weights[source, pl.ds(step * tall, tall), cut].astype(F32)
                slots[slot, :, cut] = (product[:, cut] + factor * value).astype(BF16)
            copy = pltpu.make_async_copy(
                slots.at[slot], out.at[source, pl.ds(step * tall, tall)], sems.at[slot]
            )
            copy.start()
            pending[slot] = copy
    for copy in pending:
        if copy is not None:
            copy.wait()


def encoder_grad_kernel(layers, loss_scale, tall, ordered, acts, norms, *refs):
    main_parts, last_parts = refs[:layers], refs[layers : 2 * layers]
    out, sums_out, low, slots, sems = refs[2 * layers :]
    target = lax.axis_index("layer")
    features = main_parts[0].shape[1]
    place = pl.ds(pl.multiple_of(target * features, features), features)
    shift = norms[pl.ds(target, 1), :] * loss_scale
    sums = jnp.zeros((1, features), F32)
    start = 0
    for parts in (main_parts, last_parts):
        total = parts[0][...]
        rows = pl.ds(start, total.shape[0])
        start += total.shape[0]
        for part in parts[1:]:
            total = total + part[...].astype(F32)
        grad = jnp.where(acts[rows, place] > 0, total + shift, 0.0)
        sums = sums + jnp.sum(grad, axis=0, keepdims=True)
        low[rows, :] = grad.astype(BF16)
    sums_out[...] = sums
    width = ordered.shape[0]
    copies = []
    for step in range(width // tall):
        rows = pl.ds(step * tall, tall)
        slots[rows, :] = jnp.dot(
            ordered[rows, :], low[...], preferred_element_type=F32
        ).astype(BF16)
        copy = pltpu.make_async_copy(slots.at[rows], out.at[rows], sems.at[step])
        copy.start()
        copies.append(copy)
    for copy in copies:
        copy.wait()


def on_device(
    layer_inputs,
    layer_targets,
    row_order,
    encoder_weight,
    encoder_bias,
    decoder_weight,
    decoder_bias,
):
    layers = lax.axis_size("layer")
    ranks = lax.axis_size("tok")
    lines = ranks // 2
    row_total = row_order.shape[0]
    height = row_total // ranks
    loss_scale = 1.0 / math.sqrt(row_total)
    weights = decoder_weight[0]
    features, width = weights.shape[1:]
    last = 2 * height
    first = row_total - last
    groups = (range(lines - 1), range(lines - 1, lines))
    hbm = pl.BlockSpec(memory_space=pltpu.HBM)
    struct = jax.ShapeDtypeStruct
    block_flops = 2 * row_total * features * width

    def swap_tok(value, step):
        return lax.ppermute(value, "tok", [(i, i ^ step) for i in range(ranks)])

    def swap_layer(value, step):
        return lax.ppermute(value, "layer", [(i, i ^ step) for i in range(layers)])

    def gather_lines(own, before=()):
        lane = {0: own}
        for line in sorted(range(1, lines), key=lambda j: (bin(j).count("1"), j)):
            low = line & -line
            lane[line] = swap_tok(lane[line ^ low], 2 * low)
        here, *_ = lax.optimization_barrier((own, *before)) if before else (own,)
        main = [lane[j] for j in groups[0]]
        main += [swap_tok(lane[j] if j else here, 1) for j in groups[0]]
        return main, [lane[lines - 1]]

    def other_core(pieces, after):
        *pieces, _ = lax.optimization_barrier((*pieces, after))
        return pieces + [swap_tok(piece, 1) for piece in pieces]

    relative = []
    for group in groups:
        for core in range(2):
            relative += [2 * j + core for j in group]
    order = call(
        functools.partial(table_kernel, tuple(relative)),
        struct((row_total, row_total), BF16),
        whole(1),
        whole(1)[0],
        [pltpu.VMEM((row_total, row_total), F32)],
        6 * MICROSECOND,
        4 * row_total * row_total,
    )(row_order[None])

    squares = call(
        norm_kernel,
        struct((layers, features), F32),
        whole(1),
        whole(1)[0],
        [],
        4 * layers * features * width,
        2 * layers * features * width,
    )(weights)
    main_inputs, last_inputs = gather_lines(layer_inputs[0], (order, squares))
    encode_operands = (encoder_weight[0], encoder_bias)
    main_own = call(
        functools.partial(encode_kernel, len(main_inputs)),
        struct((first, features), BF16),
        whole(len(main_inputs) + 2),
        whole(1)[0],
        [pltpu.VMEM((first, width), BF16)],
        2 * first * width * features,
        2 * width * features,
    )(*main_inputs, *encode_operands)
    main_acts = [main_own] + [swap_layer(main_own, step) for step in range(1, layers)]
    last_inputs = other_core(last_inputs, main_own)
    extra = -(-3 * layers // 16) * 16
    last_own = call(
        functools.partial(encode_last_kernel, len(last_inputs)),
        struct((last + extra, features), BF16),
        whole(len(last_inputs) + 3),
        whole(1)[0],
        [pltpu.VMEM((last, width), BF16), pltpu.VMEM((extra, features), F32)],
        2 * last * width * features,
        2 * width * features,
    )(*last_inputs, *encode_operands, squares)
    last_acts = [last_own] + [swap_layer(last_own, step) for step in range(1, layers)]
    first_sorted = call(
        functools.partial(sort_kernel, layers),
        struct((row_total, layers * features), F32),
        whole(layers + 1),
        whole(1)[0],
        [],
        2 * row_total * first * layers * features,
        2 * first * layers * features,
    )(order, *main_acts)

    columns = min(512, width)
    acts_all, keep, send, norms = call(
        functools.partial(decode_kernel, layers, last, columns),
        (
            struct((row_total, layers * features), BF16),
            struct((row_total // 2, width), BF16),
            struct((row_total // 2, width), BF16),
            struct((layers, features), F32),
        ),
        whole(3 + layers),
        tuple(whole(4)),
        [],
        layers * block_flops,
        2 * layers * features * width,
    )(order, first_sorted, *last_acts, weights)

    pair = keep.astype(F32) + swap_tok(send, 1).astype(F32)
    parts = [pair[i * height : (i + 1) * height] for i in range(lines)]
    last_leaf = None
    for line in reversed(range(1, lines)):
        low = line & -line
        block = parts[line].astype(BF16)
        if low == 1 and last_leaf is not None:
            block, last_leaf = lax.optimization_barrier((block, last_leaf))
        arrived = swap_tok(block, 2 * low)
        if low == 1:
            last_leaf = arrived
        parts[line ^ low] = parts[line ^ low] + arrived.astype(F32)
    resid_full = (
        parts[0] + decoder_bias[0] - layer_targets[0].astype(F32)
    ) * loss_scale

    _, *late = lax.optimization_barrier((send, *main_inputs, *last_inputs))
    ordered = call(
        functools.partial(order_kernel, len(late)),
        struct((width, row_total), BF16),
        whole(len(late) + 1),
        whole(1)[0],
        [pltpu.VMEM((row_total, width), BF16)],
        2 * row_total * row_total * width,
        4 * row_total * width,
    )(*late, order)
    resid_low, ordered = lax.optimization_barrier((resid_full.astype(BF16), ordered))
    main_resid, last_resid = gather_lines(resid_low)

    def grad_acts(pieces):
        count = len(pieces) * height
        *parts, rows = call(
            functools.partial(grad_kernel, layers, len(pieces)),
            (
                *[struct((count, features), BF16 if step else F32) for step in range(layers)],
                struct((count, width), BF16),
            ),
            whole(len(pieces) + 1),
            tuple(whole(layers + 1)),
            [],
            2 * count * layers * features * width,
            2 * layers * features * width,
        )(*pieces, weights)
        sums = [swap_layer(parts[step], step) if step else parts[0] for step in range(layers)]
        return parts[0], sums, rows

    main_grad, main_sums, main_rows = grad_acts(main_resid)
    last_resid = other_core(last_resid, main_grad)
    _, last_sums, last_rows = grad_acts(last_resid)

    tall = math.gcd(256, features)
    decoder_grad, bias_grad = call(
        functools.partial(decoder_grad_kernel, loss_scale),
        (struct((layers, features, width), BF16), struct((1, width), F32)),
        whole(5),
        (hbm, whole(1)[0]),
        [
            pltpu.VMEM((row_total, width), BF16),
            pltpu.VMEM((4, tall, width), BF16),
            pltpu.SemaphoreType.DMA((4,)),
        ],
        layers * block_flops,
        4 * layers * features * width,
    )(acts_all, norms, main_rows, last_rows, weights)

    tall = min(512, width)
    encoder_grad, feature_grad = call(
        functools.partial(encoder_grad_kernel, layers, loss_scale, tall),
        (struct((width, features), BF16), struct((1, features), F32)),
        whole(3 + 2 * layers),
        (hbm, whole(1)[0]),
        [
            pltpu.VMEM((row_total, features), BF16),
            pltpu.VMEM((width, features), BF16),
            pltpu.SemaphoreType.DMA((width // tall,)),
        ],
        block_flops,
        2 * features * width,
    )(ordered, acts_all, norms, *main_sums, *last_sums)
    return (encoder_grad[None], feature_grad, decoder_grad[None], bias_grad)


def solution(mesh):
    placed = (
        P("layer", "tok", None),
        P("layer", "tok", None),
        P(),
        P("layer", None, "tok"),
        P("layer", "tok"),
        P("layer", None, "tok", None),
        P("layer", None),
    )
    return jax.shard_map(
        on_device,
        mesh=mesh,
        in_specs=placed,
        out_specs=(
            P("layer", None, "tok"),
            P("layer", "tok"),
            P("layer", None, "tok", None),
            P("layer", None),
        ),
        check_vma=False,
    )
```

```python
import functools
import math

import jax
import jax.numpy as jnp
from jax import lax
from jax.experimental import pallas as pl
from jax.experimental.pallas import tpu as pltpu
from jax.sharding import PartitionSpec as P

BF16 = jnp.bfloat16
F32 = jnp.float32
VMEM_LIMIT = 16 * 1024 * 1024
MICROSECOND = 1_150_000_000


def whole(count):
    return [pl.BlockSpec(memory_space=pltpu.VMEM)] * count


def call(kernel, out_shape, in_specs, out_specs, scratch, flops, moved, limit=VMEM_LIMIT):
    return pl.pallas_call(
        kernel,
        out_shape=out_shape,
        in_specs=in_specs,
        out_specs=out_specs,
        scratch_shapes=scratch,
        compiler_params=pltpu.CompilerParams(vmem_limit_bytes=limit),
        cost_estimate=pl.CostEstimate(flops=flops, bytes_accessed=moved, transcendentals=0),
    )


def table_kernel(relative, rows_ref, order, table):
    rank = lax.axis_index("tok")
    total_rows = table.shape[0]
    height = total_rows // len(relative)
    lane = lax.broadcasted_iota(jnp.int32, (1, total_rows), 1)
    held_rows = lane % height
    for index, offset in enumerate(relative):
        held_rows = held_rows + jnp.where(lane // height == index, (rank ^ offset) * height, 0)
    wanted = jnp.broadcast_to(rows_ref[...], (total_rows, total_rows)).T
    table[...] = jnp.where(wanted == held_rows, 1.0, 0.0)
    for index, offset in enumerate(relative):
        start = pl.multiple_of((rank ^ offset) * height, height)
        order[pl.ds(index * height, height), :] = table[pl.ds(start, height), :].astype(BF16)


def norm_kernel(weights, after, squares):
    layers, features, width = weights.shape
    target = lax.axis_index("layer")
    for source in range(layers):
        total = jnp.zeros((features, 128), F32)
        for part in range(width // 128):
            value = weights[source, :, pl.ds(part * 128, 128)].astype(F32)
            total = total + value * value
        column = jnp.sum(total, axis=1, keepdims=True)
        row = jnp.broadcast_to(column, (features, 128)).T[:1]
        squares[pl.ds(source, 1), :] = jnp.where(source <= target, row, 0.0)


def gather_rows(pieces, rows):
    height = pieces[0].shape[0]
    for index, piece in enumerate(pieces):
        rows[pl.ds(index * height, height), :] = piece[...]


def gather_parts(parts, rows):
    start = 0
    for part in parts:
        rows[pl.ds(start, part.shape[0]), :] = part[...]
        start += part.shape[0]


def encode_kernel(count, *refs):
    pieces, (weight, bias, out, rows) = refs[:count][::-1], refs[count:]
    gather_rows(pieces, rows)
    value = jnp.dot(rows[...], weight[...], preferred_element_type=F32) + bias[...]
    out[...] = jnp.maximum(value, 0.0).astype(BF16)


def encode_last_kernel(count, *refs):
    pieces, (weight, bias, squares, out, rows, extra) = refs[:count], refs[count:]
    gather_rows(pieces, rows)
    value = jnp.dot(rows[...], weight[...], preferred_element_type=F32) + bias[...]
    out[pl.ds(0, rows.shape[0]), :] = jnp.maximum(value, 0.0).astype(BF16)
    extra[...] = jnp.zeros(extra.shape, F32)
    rest = squares[...]
    layers = rest.shape[0]
    for part in range(3):
        term = rest.astype(BF16).astype(F32)
        extra[pl.ds(part * layers, layers), :] = term
        rest = rest - term
    out[pl.ds(rows.shape[0], extra.shape[0]), :] = extra[...].astype(BF16)


def sort_kernel(layers, order, *refs):
    acts, out = refs[:layers][::-1], refs[layers]
    target = lax.axis_index("layer")
    first, features = acts[0].shape
    for offset in range(layers):
        place = pl.ds(pl.multiple_of((target ^ offset) * features, features), features)
        out[:, place] = jnp.dot(order[:, :first], acts[offset][...], preferred_element_type=F32)


def decode_kernel(layers, last, columns, order_ref, first_sorted, *refs):
    acts, weights = refs[:layers][::-1], refs[layers]
    acts_out, keep, send, far_keep, far_send, norms = refs[layers + 1 :]
    target = lax.axis_index("layer")
    features, width = weights.shape[1:]
    total_rows = order_ref.shape[0]
    first = total_rows - last
    for offset in range(layers):
        source = target ^ offset
        place = pl.ds(pl.multiple_of(source * features, features), features)
        value = jnp.dot(
            order_ref[:, pl.ds(first, last)],
            acts[offset][pl.ds(0, last), :],
            preferred_element_type=F32,
        )
        used = jnp.where(source <= target, 1.0, 0.0)
        acts_out[:, place] = ((first_sorted[:, place] + value) * used).astype(BF16)
    near, far = first // 2, last // 2
    for part in range(width // columns):
        lanes = pl.ds(part * columns, columns)
        block = weights[:, :, lanes].reshape(layers * features, columns)
        value = jnp.dot(acts_out[...], block, preferred_element_type=F32).astype(BF16)
        keep[:, lanes] = value[:near]
        send[:, lanes] = value[near:first]
        far_keep[:, lanes] = value[first : first + far]
        far_send[:, lanes] = value[first + far :]
    total = jnp.zeros((layers, features), F32)
    for offset in range(layers):
        value = acts[offset][pl.ds(last, acts[0].shape[0] - last), :].astype(F32)
        for part in range(3):
            total = total + value[part * layers : (part + 1) * layers]
    norms[...] = jnp.sqrt(total + 1e-06)


def order_kernel(count, *refs):
    pieces, (order, weights, out, turned, rows) = refs[:count], refs[count:]
    gather_rows(pieces, rows)
    out[...] = lax.dot_general(
        rows[...], order[...], (((0,), (1,)), ((), ())), preferred_element_type=F32
    ).astype(BF16)
    for source in range(weights.shape[0]):
        turned[source] = weights[source].T


def grad_kernel(layers, count, *refs):
    pieces, turned = refs[:count][::-1], refs[count]
    outs, rows = refs[count + 1 : count + 1 + layers], refs[count + 1 + layers]
    target = lax.axis_index("layer")
    gather_rows(pieces, rows)
    for offset in range(layers):
        source = target ^ offset
        value = jnp.dot(rows[...], turned[source], preferred_element_type=F32)
        outs[offset][...] = jnp.where(source <= target, value, 0.0).astype(outs[offset].dtype)


def decoder_grad_kernel(loss_scale, acts, norms, main_rows, last_rows, weights, *refs):
    out, bias_out, rows, slots, sems = refs
    layers, features, width = weights.shape
    depth, tall = slots.shape[:2]
    steps = features // tall
    pending = [None] * depth
    gather_parts((main_rows, last_rows), rows)
    bias_out[...] = jnp.sum(rows[...].astype(F32), axis=0, keepdims=True)
    for source in range(layers):
        used = source <= lax.axis_index("layer")
        for step in range(steps):
            slot = (source * steps + step) % depth
            if pending[slot] is not None:
                pending[slot].wait()
            block = acts[:, pl.ds(source * features + step * tall, tall)]
            sums = jnp.sum(block.astype(F32), axis=0, keepdims=True)
            norm = norms[pl.ds(source, 1), pl.ds(step * tall, tall)]
            factor_row = jnp.where(used, sums * loss_scale / norm, 0.0)
            factor = jnp.broadcast_to(factor_row, (128, tall)).T
            product = lax.dot_general(
                block, rows[...], (((0,), (0,)), ((), ())), preferred_element_type=F32
            )
            for part in range(width // 128):
                cut = slice(part * 128, part * 128 + 128)
                value = weights[source, pl.ds(step * tall, tall), cut].astype(F32)
                slots[slot, :, cut] = (product[:, cut] + factor * value).astype(BF16)
            copy = pltpu.make_async_copy(
                slots.at[slot], out.at[source, pl.ds(step * tall, tall)], sems.at[slot]
            )
            copy.start()
            pending[slot] = copy
    for copy in pending:
        if copy is not None:
            copy.wait()


def encoder_grad_kernel(layers, loss_scale, tall, ordered, acts, norms, *refs):
    main_parts, last_parts = refs[:layers][::-1], refs[layers : 2 * layers][::-1]
    out, sums_out, low, slots, sems = refs[2 * layers :]
    target = lax.axis_index("layer")
    features = main_parts[0].shape[1]
    place = pl.ds(pl.multiple_of(target * features, features), features)
    shift = norms[pl.ds(target, 1), :] * loss_scale
    sums = jnp.zeros((1, features), F32)
    start = 0
    for parts in (main_parts, last_parts):
        total = parts[0][...]
        rows = pl.ds(start, total.shape[0])
        start += total.shape[0]
        for part in parts[1:]:
            total = total + part[...].astype(F32)
        grad = jnp.where(acts[rows, place] > 0, total + shift, 0.0)
        sums = sums + jnp.sum(grad, axis=0, keepdims=True)
        low[rows, :] = grad.astype(BF16)
    sums_out[...] = sums
    width = ordered.shape[0]
    copies = []
    for step in range(width // tall):
        rows = pl.ds(step * tall, tall)
        slots[rows, :] = jnp.dot(
            ordered[rows, :], low[...], preferred_element_type=F32
        ).astype(BF16)
        copy = pltpu.make_async_copy(slots.at[rows], out.at[rows], sems.at[step])
        copy.start()
        copies.append(copy)
    for copy in copies:
        copy.wait()


def on_device(
    layer_inputs,
    layer_targets,
    row_order,
    encoder_weight,
    encoder_bias,
    decoder_weight,
    decoder_bias,
):
    layers = lax.axis_size("layer")
    ranks = lax.axis_size("tok")
    lines = ranks // 2
    row_total = row_order.shape[0]
    height = row_total // ranks
    loss_scale = 1.0 / math.sqrt(row_total)
    weights = decoder_weight[0]
    features, width = weights.shape[1:]
    last = 2 * height
    first = row_total - last
    groups = (range(lines - 1), range(lines - 1, lines))
    hbm = pl.BlockSpec(memory_space=pltpu.HBM)
    struct = jax.ShapeDtypeStruct
    block_flops = 2 * row_total * features * width

    def swap_tok(value, step):
        return lax.ppermute(value, "tok", [(i, i ^ step) for i in range(ranks)])

    def swap_layer(value, step):
        return lax.ppermute(value, "layer", [(i, i ^ step) for i in range(layers)])

    def exchange(parts):
        arrived = list(parts)
        for step in reversed(range(1, layers)):
            arrived[step] = swap_layer(parts[step], step)
        return arrived

    def gather_lines(own, before=()):
        lane = {0: own}
        for line in sorted(range(1, lines), key=lambda j: (bin(j).count("1"), -j)):
            low = line & -line
            lane[line] = swap_tok(lane[line ^ low], 2 * low)
        here, *_ = lax.optimization_barrier((own, *before)) if before else (own,)
        main = [lane[j] for j in groups[0]]
        main += [swap_tok(lane[j] if j else here, 1) for j in groups[0]]
        return main, [lane[lines - 1]]

    def other_core(pieces, after):
        *pieces, _ = lax.optimization_barrier((*pieces, after))
        return pieces + [swap_tok(piece, 1) for piece in pieces]

    relative = []
    for group in groups:
        for core in range(2):
            relative += [2 * j + core for j in group]
    order = call(
        functools.partial(table_kernel, tuple(relative)),
        struct((row_total, row_total), BF16),
        whole(1),
        whole(1)[0],
        [pltpu.VMEM((row_total, row_total), F32)],
        6 * MICROSECOND,
        4 * row_total * row_total,
    )(row_order[None])

    main_inputs, last_inputs = gather_lines(layer_inputs[0], (order,))
    encode_operands = (encoder_weight[0], encoder_bias)
    main_own = call(
        functools.partial(encode_kernel, len(main_inputs)),
        struct((first, features), BF16),
        whole(len(main_inputs) + 2),
        whole(1)[0],
        [pltpu.VMEM((first, width), BF16)],
        2 * first * width * features,
        2 * width * features,
    )(*main_inputs[::-1], *encode_operands)
    main_acts = exchange([main_own] * layers)
    squares = call(
        norm_kernel,
        struct((layers, features), F32),
        whole(2),
        whole(1)[0],
        [],
        4 * layers * features * width,
        2 * layers * features * width,
    )(weights, main_own)
    last_inputs = other_core(last_inputs, main_own)
    extra = -(-3 * layers // 16) * 16
    last_own = call(
        functools.partial(encode_last_kernel, len(last_inputs)),
        struct((last + extra, features), BF16),
        whole(len(last_inputs) + 3),
        whole(1)[0],
        [pltpu.VMEM((last, width), BF16), pltpu.VMEM((extra, features), F32)],
        2 * last * width * features,
        2 * width * features,
    )(*last_inputs, *encode_operands, squares)
    last_acts = exchange([last_own] * layers)
    first_sorted = call(
        functools.partial(sort_kernel, layers),
        struct((row_total, layers * features), F32),
        whole(layers + 1),
        whole(1)[0],
        [],
        2 * row_total * first * layers * features,
        2 * first * layers * features,
    )(order, *main_acts[::-1])

    columns = min(512, width)
    acts_all, keep, send, far_keep, far_send, norms = call(
        functools.partial(decode_kernel, layers, last, columns),
        (
            struct((row_total, layers * features), BF16),
            *[struct((first // 2, width), BF16)] * 2,
            *[struct((last // 2, width), BF16)] * 2,
            struct((layers, features), F32),
        ),
        whole(3 + layers),
        tuple(whole(6)),
        [],
        layers * block_flops,
        2 * layers * features * width,
    )(order, first_sorted, *last_acts[::-1], weights)

    far = far_keep.astype(F32) + swap_tok(far_send, 1).astype(F32)
    near = keep.astype(F32) + swap_tok(send, 1).astype(F32)
    parts = [near[i * height : (i + 1) * height] for i in range(lines - 1)] + [far]
    last_leaf = None
    for line in reversed(range(1, lines)):
        low = line & -line
        block = parts[line].astype(BF16)
        if low == 1 and last_leaf is not None:
            block, last_leaf = lax.optimization_barrier((block, last_leaf))
        arrived = swap_tok(block, 2 * low)
        if low == 1:
            last_leaf = arrived
        parts[line ^ low] = parts[line ^ low] + arrived.astype(F32)
    resid_full = (
        parts[0] + decoder_bias[0] - layer_targets[0].astype(F32)
    ) * loss_scale

    _, *late = lax.optimization_barrier((send, *main_inputs, *last_inputs))
    ordered, turned = call(
        functools.partial(order_kernel, len(late)),
        (struct((width, row_total), BF16), struct((layers, width, features), BF16)),
        whole(len(late) + 2),
        tuple(whole(2)),
        [pltpu.VMEM((row_total, width), BF16)],
        2 * row_total * row_total * width,
        4 * layers * features * width,
    )(*late, order, weights)
    resid_low, ordered, turned = lax.optimization_barrier(
        (resid_full.astype(BF16), ordered, turned)
    )
    main_resid, last_resid = gather_lines(resid_low)

    def grad_acts(pieces):
        count = len(pieces) * height
        *parts, rows = call(
            functools.partial(grad_kernel, layers, len(pieces)),
            (
                *[struct((count, features), BF16 if step else F32) for step in range(layers)],
                struct((count, width), BF16),
            ),
            whole(len(pieces) + 1),
            tuple(whole(layers + 1)),
            [],
            2 * count * layers * features * width,
            2 * layers * features * width,
        )(*pieces[::-1], turned)
        return parts[0], exchange(parts), rows

    main_grad, main_sums, main_rows = grad_acts(main_resid)
    last_resid = other_core(last_resid, main_grad)
    _, last_sums, last_rows = grad_acts(last_resid)

    tall = math.gcd(256, features)
    decoder_grad, bias_grad = call(
        functools.partial(decoder_grad_kernel, loss_scale),
        (struct((layers, features, width), BF16), struct((1, width), F32)),
        whole(5),
        (hbm, whole(1)[0]),
        [
            pltpu.VMEM((row_total, width), BF16),
            pltpu.VMEM((4, tall, width), BF16),
            pltpu.SemaphoreType.DMA((4,)),
        ],
        layers * block_flops,
        4 * layers * features * width,
    )(acts_all, norms, main_rows, last_rows, weights)

    tall = min(512, width)
    encoder_grad, feature_grad = call(
        functools.partial(encoder_grad_kernel, layers, loss_scale, tall),
        (struct((width, features), BF16), struct((1, features), F32)),
        whole(3 + 2 * layers),
        (hbm, whole(1)[0]),
        [
            pltpu.VMEM((row_total, features), BF16),
            pltpu.VMEM((width, features), BF16),
            pltpu.SemaphoreType.DMA((width // tall,)),
        ],
        block_flops,
        2 * features * width,
    )(ordered, acts_all, norms, *main_sums[::-1], *last_sums[::-1])
    return (encoder_grad[None], feature_grad, decoder_grad[None], bias_grad)


def solution(mesh):
    placed = (
        P("layer", "tok", None),
        P("layer", "tok", None),
        P(),
        P("layer", None, "tok"),
        P("layer", "tok"),
        P("layer", None, "tok", None),
        P("layer", None),
    )
    return jax.shard_map(
        on_device,
        mesh=mesh,
        in_specs=placed,
        out_specs=(
            P("layer", None, "tok"),
            P("layer", "tok"),
            P("layer", None, "tok", None),
            P("layer", None),
        ),
        check_vma=False,
    )
```

```python
import functools
import math

import jax
import jax.numpy as jnp
from jax import lax
from jax.experimental import pallas as pl
from jax.experimental.pallas import tpu as pltpu
from jax.sharding import PartitionSpec as P

BF16 = jnp.bfloat16
F32 = jnp.float32
VMEM_LIMIT = 16 * 1024 * 1024
MICROSECOND = 1_150_000_000


def whole(count):
    return [pl.BlockSpec(memory_space=pltpu.VMEM)] * count


def call(kernel, out_shape, in_specs, out_specs, scratch, flops, moved, limit=VMEM_LIMIT):
    return pl.pallas_call(
        kernel,
        out_shape=out_shape,
        in_specs=in_specs,
        out_specs=out_specs,
        scratch_shapes=scratch,
        compiler_params=pltpu.CompilerParams(vmem_limit_bytes=limit),
        cost_estimate=pl.CostEstimate(flops=flops, bytes_accessed=moved, transcendentals=0),
    )


def table_kernel(relative, rows_ref, order, table):
    rank = lax.axis_index("tok")
    total_rows = table.shape[0]
    height = total_rows // len(relative)
    lane = lax.broadcasted_iota(jnp.int32, (1, total_rows), 1)
    held_rows = lane % height
    for index, offset in enumerate(relative):
        held_rows = held_rows + jnp.where(lane // height == index, (rank ^ offset) * height, 0)
    wanted = jnp.broadcast_to(rows_ref[...], (total_rows, total_rows)).T
    table[...] = jnp.where(wanted == held_rows, 1.0, 0.0)
    for index, offset in enumerate(relative):
        start = pl.multiple_of((rank ^ offset) * height, height)
        order[pl.ds(index * height, height), :] = table[pl.ds(start, height), :].astype(BF16)


def norm_kernel(weights, after, squares):
    layers, features, width = weights.shape
    target = lax.axis_index("layer")
    for source in range(layers):
        total = jnp.zeros((features, 128), F32)
        for part in range(width // 128):
            value = weights[source, :, pl.ds(part * 128, 128)].astype(F32)
            total = total + value * value
        column = jnp.sum(total, axis=1, keepdims=True)
        row = jnp.broadcast_to(column, (features, 128)).T[:1]
        squares[pl.ds(source, 1), :] = jnp.where(source <= target, row, 0.0)


def gather_rows(pieces, rows):
    height = pieces[0].shape[0]
    for index, piece in enumerate(pieces):
        rows[pl.ds(index * height, height), :] = piece[...]


def gather_parts(parts, rows):
    start = 0
    for part in parts:
        rows[pl.ds(start, part.shape[0]), :] = part[...]
        start += part.shape[0]


def encode_kernel(count, *refs):
    pieces, (weight, bias, out, rows) = refs[:count][::-1], refs[count:]
    gather_rows(pieces, rows)
    value = jnp.dot(rows[...], weight[...], preferred_element_type=F32) + bias[...]
    out[...] = jnp.maximum(value, 0.0).astype(BF16)


def encode_last_kernel(count, *refs):
    pieces, (weight, bias, squares, out, rows, extra) = refs[:count], refs[count:]
    gather_rows(pieces, rows)
    value = jnp.dot(rows[...], weight[...], preferred_element_type=F32) + bias[...]
    out[pl.ds(0, rows.shape[0]), :] = jnp.maximum(value, 0.0).astype(BF16)
    extra[...] = jnp.zeros(extra.shape, F32)
    rest = squares[...]
    layers = rest.shape[0]
    for part in range(3):
        term = rest.astype(BF16).astype(F32)
        extra[pl.ds(part * layers, layers), :] = term
        rest = rest - term
    out[pl.ds(rows.shape[0], extra.shape[0]), :] = extra[...].astype(BF16)


def sort_kernel(layers, order, *refs):
    acts, out = refs[:layers][::-1], refs[layers]
    target = lax.axis_index("layer")
    first, features = acts[0].shape
    for offset in range(layers):
        place = pl.ds(pl.multiple_of((target ^ offset) * features, features), features)
        out[:, place] = jnp.dot(order[:, :first], acts[offset][...], preferred_element_type=F32)


def decode_kernel(layers, last, columns, order_ref, first_sorted, *refs):
    acts, weights = refs[:layers][::-1], refs[layers]
    acts_out, keep, send, far_keep, far_send, norms = refs[layers + 1 :]
    target = lax.axis_index("layer")
    features, width = weights.shape[1:]
    total_rows = order_ref.shape[0]
    first = total_rows - last
    for offset in range(layers):
        source = target ^ offset
        place = pl.ds(pl.multiple_of(source * features, features), features)
        value = jnp.dot(
            order_ref[:, pl.ds(first, last)],
            acts[offset][pl.ds(0, last), :],
            preferred_element_type=F32,
        )
        used = jnp.where(source <= target, 1.0, 0.0)
        acts_out[:, place] = ((first_sorted[:, place] + value) * used).astype(BF16)
    near, far = first // 2, last // 2
    for part in range(width // columns):
        lanes = pl.ds(part * columns, columns)
        block = weights[:, :, lanes].reshape(layers * features, columns)
        value = jnp.dot(acts_out[...], block, preferred_element_type=F32).astype(BF16)
        keep[:, lanes] = value[:near]
        send[:, lanes] = value[near:first]
        far_keep[:, lanes] = value[first : first + far]
        far_send[:, lanes] = value[first + far :]
    total = jnp.zeros((layers, features), F32)
    for offset in range(layers):
        value = acts[offset][pl.ds(last, acts[0].shape[0] - last), :].astype(F32)
        for part in range(3):
            total = total + value[part * layers : (part + 1) * layers]
    norms[...] = jnp.sqrt(total + 1e-06)


def order_kernel(count, *refs):
    pieces, (order, weights, out, turned, rows) = refs[:count], refs[count:]
    gather_rows(pieces, rows)
    out[...] = lax.dot_general(
        rows[...], order[...], (((0,), (1,)), ((), ())), preferred_element_type=F32
    ).astype(BF16)
    for source in range(weights.shape[0]):
        turned[source] = weights[source].T


def grad_kernel(layers, count, *refs):
    pieces, turned = refs[:count][::-1], refs[count]
    outs, rows = refs[count + 1 : count + 1 + layers], refs[count + 1 + layers]
    target = lax.axis_index("layer")
    gather_rows(pieces, rows)
    for offset in range(layers):
        source = target ^ offset
        value = jnp.dot(rows[...], turned[source], preferred_element_type=F32)
        outs[offset][...] = jnp.where(source <= target, value, 0.0).astype(outs[offset].dtype)


def decoder_grad_kernel(loss_scale, acts, norms, main_rows, last_rows, weights, *refs):
    out, bias_out, rows, slots, sems = refs
    layers, features, width = weights.shape
    depth, tall = slots.shape[:2]
    steps = features // tall
    pending = [None] * depth
    gather_parts((main_rows, last_rows), rows)
    bias_out[...] = jnp.sum(rows[...].astype(F32), axis=0, keepdims=True)
    for source in range(layers):
        used = source <= lax.axis_index("layer")
        for step in range(steps):
            slot = (source * steps + step) % depth
            if pending[slot] is not None:
                pending[slot].wait()
            block = acts[:, pl.ds(source * features + step * tall, tall)]
            sums = jnp.sum(block.astype(F32), axis=0, keepdims=True)
            norm = norms[pl.ds(source, 1), pl.ds(step * tall, tall)]
            factor_row = jnp.where(used, sums * loss_scale / norm, 0.0)
            factor = jnp.broadcast_to(factor_row, (128, tall)).T
            product = lax.dot_general(
                block, rows[...], (((0,), (0,)), ((), ())), preferred_element_type=F32
            )
            for part in range(width // 128):
                cut = slice(part * 128, part * 128 + 128)
                value = weights[source, pl.ds(step * tall, tall), cut].astype(F32)
                slots[slot, :, cut] = (product[:, cut] + factor * value).astype(BF16)
            copy = pltpu.make_async_copy(
                slots.at[slot], out.at[source, pl.ds(step * tall, tall)], sems.at[slot]
            )
            copy.start()
            pending[slot] = copy
    for copy in pending:
        if copy is not None:
            copy.wait()


def encoder_grad_kernel(layers, loss_scale, tall, ordered, acts, norms, *refs):
    main_parts, last_parts = refs[:layers][::-1], refs[layers : 2 * layers][::-1]
    out, sums_out, low, slots, sems = refs[2 * layers :]
    target = lax.axis_index("layer")
    features = main_parts[0].shape[1]
    place = pl.ds(pl.multiple_of(target * features, features), features)
    shift = norms[pl.ds(target, 1), :] * loss_scale
    sums = jnp.zeros((1, features), F32)
    start = 0
    for parts in (main_parts, last_parts):
        total = parts[0][...]
        rows = pl.ds(start, total.shape[0])
        start += total.shape[0]
        for part in parts[1:]:
            total = total + part[...].astype(F32)
        grad = jnp.where(acts[rows, place] > 0, total + shift, 0.0)
        sums = sums + jnp.sum(grad, axis=0, keepdims=True)
        low[rows, :] = grad.astype(BF16)
    sums_out[...] = sums
    width = ordered.shape[0]
    copies = []
    for step in range(width // tall):
        rows = pl.ds(step * tall, tall)
        slots[rows, :] = jnp.dot(
            ordered[rows, :], low[...], preferred_element_type=F32
        ).astype(BF16)
        copy = pltpu.make_async_copy(slots.at[rows], out.at[rows], sems.at[step])
        copy.start()
        copies.append(copy)
    for copy in copies:
        copy.wait()


def on_device(
    layer_inputs,
    layer_targets,
    row_order,
    encoder_weight,
    encoder_bias,
    decoder_weight,
    decoder_bias,
):
    layers = lax.axis_size("layer")
    ranks = lax.axis_size("tok")
    lines = ranks // 2
    row_total = row_order.shape[0]
    height = row_total // ranks
    loss_scale = 1.0 / math.sqrt(row_total)
    weights = decoder_weight[0]
    features, width = weights.shape[1:]
    last = 2 * height
    first = row_total - last
    groups = (range(lines - 1), range(lines - 1, lines))
    hbm = pl.BlockSpec(memory_space=pltpu.HBM)
    struct = jax.ShapeDtypeStruct
    block_flops = 2 * row_total * features * width

    def swap_tok(value, step):
        return lax.ppermute(value, "tok", [(i, i ^ step) for i in range(ranks)])

    def swap_layer(value, step):
        return lax.ppermute(value, "layer", [(i, i ^ step) for i in range(layers)])

    def exchange(parts):
        arrived = list(parts)
        for step in reversed(range(1, layers)):
            arrived[step] = swap_layer(parts[step], step)
        return arrived

    def gather_lines(own, before=()):
        lane = {0: own}
        for line in sorted(range(1, lines), key=lambda j: (bin(j).count("1"), -j)):
            low = line & -line
            lane[line] = swap_tok(lane[line ^ low], 2 * low)
        here, *_ = lax.optimization_barrier((own, *before)) if before else (own,)
        main = [lane[j] for j in groups[0]]
        main += [swap_tok(lane[j] if j else here, 1) for j in groups[0]]
        return main, [lane[lines - 1]]

    def other_core(pieces, after):
        *pieces, _ = lax.optimization_barrier((*pieces, after))
        return pieces + [swap_tok(piece, 1) for piece in pieces]

    relative = []
    for group in groups:
        for core in range(2):
            relative += [2 * j + core for j in group]
    order = call(
        functools.partial(table_kernel, tuple(relative)),
        struct((row_total, row_total), BF16),
        whole(1),
        whole(1)[0],
        [pltpu.VMEM((row_total, row_total), F32)],
        6 * MICROSECOND,
        4 * row_total * row_total,
    )(row_order[None])

    main_inputs, last_inputs = gather_lines(layer_inputs[0], (order,))
    encode_operands = (encoder_weight[0], encoder_bias)
    main_own = call(
        functools.partial(encode_kernel, len(main_inputs)),
        struct((first, features), BF16),
        whole(len(main_inputs) + 2),
        whole(1)[0],
        [pltpu.VMEM((first, width), BF16)],
        2 * first * width * features,
        2 * width * features,
    )(*main_inputs[::-1], *encode_operands)
    main_acts = exchange([main_own] * layers)
    squares = call(
        norm_kernel,
        struct((layers, features), F32),
        whole(2),
        whole(1)[0],
        [],
        4 * layers * features * width,
        2 * layers * features * width,
    )(weights, main_own)
    last_inputs = other_core(last_inputs, squares)
    extra = -(-3 * layers // 16) * 16
    last_own = call(
        functools.partial(encode_last_kernel, len(last_inputs)),
        struct((last + extra, features), BF16),
        whole(len(last_inputs) + 3),
        whole(1)[0],
        [pltpu.VMEM((last, width), BF16), pltpu.VMEM((extra, features), F32)],
        2 * last * width * features,
        2 * width * features,
    )(*last_inputs, *encode_operands, squares)
    last_acts = exchange([last_own] * layers)
    first_sorted = call(
        functools.partial(sort_kernel, layers),
        struct((row_total, layers * features), F32),
        whole(layers + 1),
        whole(1)[0],
        [],
        2 * row_total * first * layers * features,
        2 * first * layers * features,
    )(order, *main_acts[::-1])

    columns = min(512, width)
    acts_all, keep, send, far_keep, far_send, norms = call(
        functools.partial(decode_kernel, layers, last, columns),
        (
            struct((row_total, layers * features), BF16),
            *[struct((first // 2, width), BF16)] * 2,
            *[struct((last // 2, width), BF16)] * 2,
            struct((layers, features), F32),
        ),
        whole(3 + layers),
        tuple(whole(6)),
        [],
        layers * block_flops,
        2 * layers * features * width,
    )(order, first_sorted, *last_acts[::-1], weights)

    far = far_keep.astype(F32) + swap_tok(far_send, 1).astype(F32)
    near = keep.astype(F32) + swap_tok(send, 1).astype(F32)
    parts = [near[i * height : (i + 1) * height] for i in range(lines - 1)] + [far]
    blocks = {}
    for line in reversed(range(1, lines)):
        low = line & -line
        blocks[line] = parts[line].astype(BF16)
        if low == 1 and line + 1 in blocks:
            blocks[line], _ = lax.optimization_barrier((blocks[line], blocks[line + 1]))
        arrived = swap_tok(blocks[line], 2 * low)
        parts[line ^ low] = parts[line ^ low] + arrived.astype(F32)
    resid_full = (
        parts[0] + decoder_bias[0] - layer_targets[0].astype(F32)
    ) * loss_scale

    _, *late = lax.optimization_barrier((send, *main_inputs, *last_inputs))
    ordered, turned = call(
        functools.partial(order_kernel, len(late)),
        (struct((width, row_total), BF16), struct((layers, width, features), BF16)),
        whole(len(late) + 2),
        tuple(whole(2)),
        [pltpu.VMEM((row_total, width), BF16)],
        2 * row_total * row_total * width,
        4 * layers * features * width,
    )(*late, order, weights)
    resid_low, ordered, turned = lax.optimization_barrier(
        (resid_full.astype(BF16), ordered, turned)
    )
    main_resid, last_resid = gather_lines(resid_low)

    def grad_acts(pieces):
        count = len(pieces) * height
        *parts, rows = call(
            functools.partial(grad_kernel, layers, len(pieces)),
            (
                *[struct((count, features), BF16 if step else F32) for step in range(layers)],
                struct((count, width), BF16),
            ),
            whole(len(pieces) + 1),
            tuple(whole(layers + 1)),
            [],
            2 * count * layers * features * width,
            2 * layers * features * width,
        )(*pieces[::-1], turned)
        return parts[0], exchange(parts), rows

    main_grad, main_sums, main_rows = grad_acts(main_resid)
    last_resid = other_core(last_resid, main_grad)
    _, last_sums, last_rows = grad_acts(last_resid)

    tall = math.gcd(256, features)
    slots = min(8, layers * features // tall)
    decoder_grad, bias_grad = call(
        functools.partial(decoder_grad_kernel, loss_scale),
        (struct((layers, features, width), BF16), struct((1, width), F32)),
        whole(5),
        (hbm, whole(1)[0]),
        [
            pltpu.VMEM((row_total, width), BF16),
            pltpu.VMEM((slots, tall, width), BF16),
            pltpu.SemaphoreType.DMA((slots,)),
        ],
        layers * block_flops,
        4 * layers * features * width,
    )(acts_all, norms, main_rows, last_rows, weights)

    tall = min(512, width)
    encoder_grad, feature_grad = call(
        functools.partial(encoder_grad_kernel, layers, loss_scale, tall),
        (struct((width, features), BF16), struct((1, features), F32)),
        whole(3 + 2 * layers),
        (hbm, whole(1)[0]),
        [
            pltpu.VMEM((row_total, features), BF16),
            pltpu.VMEM((width, features), BF16),
            pltpu.SemaphoreType.DMA((width // tall,)),
        ],
        block_flops,
        2 * features * width,
    )(ordered, acts_all, norms, *main_sums[::-1], *last_sums[::-1])
    return (encoder_grad[None], feature_grad, decoder_grad[None], bias_grad)


def solution(mesh):
    placed = (
        P("layer", "tok", None),
        P("layer", "tok", None),
        P(),
        P("layer", None, "tok"),
        P("layer", "tok"),
        P("layer", None, "tok", None),
        P("layer", None),
    )
    return jax.shard_map(
        on_device,
        mesh=mesh,
        in_specs=placed,
        out_specs=(
            P("layer", None, "tok"),
            P("layer", "tok"),
            P("layer", None, "tok", None),
            P("layer", None),
        ),
        check_vma=False,
    )
```

```python
import functools
import math

import jax
import jax.numpy as jnp
from jax import lax
from jax.experimental import pallas as pl
from jax.experimental.pallas import tpu as pltpu
from jax.sharding import PartitionSpec as P

BF16 = jnp.bfloat16
F32 = jnp.float32
VMEM_LIMIT = 16 * 1024 * 1024
MICROSECOND = 1_150_000_000


def whole(count):
    return [pl.BlockSpec(memory_space=pltpu.VMEM)] * count


def call(kernel, out_shape, in_specs, out_specs, scratch, flops, moved, limit=VMEM_LIMIT):
    return pl.pallas_call(
        kernel,
        out_shape=out_shape,
        in_specs=in_specs,
        out_specs=out_specs,
        scratch_shapes=scratch,
        compiler_params=pltpu.CompilerParams(vmem_limit_bytes=limit),
        cost_estimate=pl.CostEstimate(flops=flops, bytes_accessed=moved, transcendentals=0),
    )


def table_kernel(relative, rows_ref, order, table):
    rank = lax.axis_index("tok")
    total_rows = table.shape[0]
    height = total_rows // len(relative)
    lane = lax.broadcasted_iota(jnp.int32, (1, total_rows), 1)
    held_rows = lane % height
    for index, offset in enumerate(relative):
        held_rows = held_rows + jnp.where(lane // height == index, (rank ^ offset) * height, 0)
    wanted = jnp.broadcast_to(rows_ref[...], (total_rows, total_rows)).T
    table[...] = jnp.where(wanted == held_rows, 1.0, 0.0)
    for index, offset in enumerate(relative):
        start = pl.multiple_of((rank ^ offset) * height, height)
        order[pl.ds(index * height, height), :] = table[pl.ds(start, height), :].astype(BF16)


def norm_kernel(weights, after, squares):
    layers, features, width = weights.shape
    target = lax.axis_index("layer")
    for source in range(layers):
        total = jnp.zeros((features, 128), F32)
        for part in range(width // 128):
            value = weights[source, :, pl.ds(part * 128, 128)].astype(F32)
            total = total + value * value
        column = jnp.sum(total, axis=1, keepdims=True)
        row = jnp.broadcast_to(column, (features, 128)).T[:1]
        squares[pl.ds(source, 1), :] = jnp.where(source <= target, row, 0.0)


def gather_rows(pieces, rows):
    height = pieces[0].shape[0]
    for index, piece in enumerate(pieces):
        rows[pl.ds(index * height, height), :] = piece[...]


def gather_parts(parts, rows):
    start = 0
    for part in parts:
        rows[pl.ds(start, part.shape[0]), :] = part[...]
        start += part.shape[0]


def encode_kernel(count, *refs):
    pieces, (weight, bias, out, rows) = refs[:count][::-1], refs[count:]
    gather_rows(pieces, rows)
    value = jnp.dot(rows[...], weight[...], preferred_element_type=F32) + bias[...]
    out[...] = jnp.maximum(value, 0.0).astype(BF16)


def encode_last_kernel(count, *refs):
    pieces, (weight, bias, squares, out, rows, extra) = refs[:count], refs[count:]
    gather_rows(pieces, rows)
    value = jnp.dot(rows[...], weight[...], preferred_element_type=F32) + bias[...]
    out[pl.ds(0, rows.shape[0]), :] = jnp.maximum(value, 0.0).astype(BF16)
    extra[...] = jnp.zeros(extra.shape, F32)
    rest = squares[...]
    layers = rest.shape[0]
    for part in range(3):
        term = rest.astype(BF16).astype(F32)
        extra[pl.ds(part * layers, layers), :] = term
        rest = rest - term
    out[pl.ds(rows.shape[0], extra.shape[0]), :] = extra[...].astype(BF16)


def sort_kernel(layers, order, *refs):
    acts, out = refs[:layers][::-1], refs[layers]
    target = lax.axis_index("layer")
    first, features = acts[0].shape
    for offset in range(layers):
        place = pl.ds(pl.multiple_of((target ^ offset) * features, features), features)
        out[:, place] = jnp.dot(order[:, :first], acts[offset][...], preferred_element_type=F32)


def decode_kernel(layers, last, columns, order_ref, first_sorted, *refs):
    acts, weights = refs[:layers][::-1], refs[layers]
    acts_out, keep, send, far_keep, far_send, norms = refs[layers + 1 :]
    target = lax.axis_index("layer")
    features, width = weights.shape[1:]
    total_rows = order_ref.shape[0]
    first = total_rows - last
    for offset in range(layers):
        source = target ^ offset
        place = pl.ds(pl.multiple_of(source * features, features), features)
        value = jnp.dot(
            order_ref[:, pl.ds(first, last)],
            acts[offset][pl.ds(0, last), :],
            preferred_element_type=F32,
        )
        used = jnp.where(source <= target, 1.0, 0.0)
        acts_out[:, place] = ((first_sorted[:, place] + value) * used).astype(BF16)
    near, far = first // 2, last // 2
    for part in range(width // columns):
        lanes = pl.ds(part * columns, columns)
        block = weights[:, :, lanes].reshape(layers * features, columns)
        value = jnp.dot(acts_out[...], block, preferred_element_type=F32).astype(BF16)
        keep[:, lanes] = value[:near]
        send[:, lanes] = value[near:first]
        far_keep[:, lanes] = value[first : first + far]
        far_send[:, lanes] = value[first + far :]
    total = jnp.zeros((layers, features), F32)
    for offset in range(layers):
        value = acts[offset][pl.ds(last, acts[0].shape[0] - last), :].astype(F32)
        for part in range(3):
            total = total + value[part * layers : (part + 1) * layers]
    norms[...] = jnp.sqrt(total + 1e-06)


def order_kernel(count, *refs):
    pieces, (order, weights, out, turned, rows) = refs[:count], refs[count:]
    gather_rows(pieces, rows)
    out[...] = lax.dot_general(
        rows[...], order[...], (((0,), (1,)), ((), ())), preferred_element_type=F32
    ).astype(BF16)
    for source in range(weights.shape[0]):
        turned[source] = weights[source].T


def grad_kernel(layers, count, *refs):
    pieces, turned = refs[:count][::-1], refs[count]
    outs, rows = refs[count + 1 : count + 1 + layers], refs[count + 1 + layers]
    target = lax.axis_index("layer")
    gather_rows(pieces, rows)
    for offset in range(layers):
        source = target ^ offset
        value = jnp.dot(rows[...], turned[source], preferred_element_type=F32)
        outs[offset][...] = jnp.where(source <= target, value, 0.0).astype(outs[offset].dtype)


def decoder_grad_kernel(loss_scale, acts, norms, main_rows, last_rows, weights, *refs):
    out, bias_out, rows, slots, sems = refs
    layers, features, width = weights.shape
    depth, tall = slots.shape[:2]
    steps = features // tall
    pending = [None] * depth
    gather_parts((main_rows, last_rows), rows)
    ones = jnp.ones((16, rows.shape[0]), BF16)
    bias_out[...] = jnp.dot(ones, rows[...], preferred_element_type=F32)[:1]
    for source in range(layers):
        used = source <= lax.axis_index("layer")
        for step in range(steps):
            slot = (source * steps + step) % depth
            if pending[slot] is not None:
                pending[slot].wait()
            block = acts[:, pl.ds(source * features + step * tall, tall)]
            sums = jnp.sum(block.astype(F32), axis=0, keepdims=True)
            norm = norms[pl.ds(source, 1), pl.ds(step * tall, tall)]
            factor_row = jnp.where(used, sums * loss_scale / norm, 0.0)
            factor = jnp.broadcast_to(factor_row, (128, tall)).T
            product = lax.dot_general(
                block, rows[...], (((0,), (0,)), ((), ())), preferred_element_type=F32
            )
            for part in range(width // 128):
                cut = slice(part * 128, part * 128 + 128)
                value = weights[source, pl.ds(step * tall, tall), cut].astype(F32)
                slots[slot, :, cut] = (product[:, cut] + factor * value).astype(BF16)
            copy = pltpu.make_async_copy(
                slots.at[slot], out.at[source, pl.ds(step * tall, tall)], sems.at[slot]
            )
            copy.start()
            pending[slot] = copy
    for copy in pending:
        if copy is not None:
            copy.wait()


def encoder_grad_kernel(layers, loss_scale, tall, ordered, acts, norms, *refs):
    main_parts, last_parts = refs[:layers][::-1], refs[layers : 2 * layers][::-1]
    out, sums_out, low, slots, sems = refs[2 * layers :]
    target = lax.axis_index("layer")
    features = main_parts[0].shape[1]
    place = pl.ds(pl.multiple_of(target * features, features), features)
    shift = norms[pl.ds(target, 1), :] * loss_scale
    sums = jnp.zeros((1, features), F32)
    start = 0
    for parts in (main_parts, last_parts):
        total = parts[0][...]
        rows = pl.ds(start, total.shape[0])
        start += total.shape[0]
        for part in parts[1:]:
            total = total + part[...].astype(F32)
        grad = jnp.where(acts[rows, place] > 0, total + shift, 0.0)
        sums = sums + jnp.sum(grad, axis=0, keepdims=True)
        low[rows, :] = grad.astype(BF16)
    sums_out[...] = sums
    width = ordered.shape[0]
    copies = []
    for step in range(width // tall):
        rows = pl.ds(step * tall, tall)
        slots[rows, :] = jnp.dot(
            ordered[rows, :], low[...], preferred_element_type=F32
        ).astype(BF16)
        copy = pltpu.make_async_copy(slots.at[rows], out.at[rows], sems.at[step])
        copy.start()
        copies.append(copy)
    for copy in copies:
        copy.wait()


def on_device(
    layer_inputs,
    layer_targets,
    row_order,
    encoder_weight,
    encoder_bias,
    decoder_weight,
    decoder_bias,
):
    layers = lax.axis_size("layer")
    ranks = lax.axis_size("tok")
    lines = ranks // 2
    row_total = row_order.shape[0]
    height = row_total // ranks
    loss_scale = 1.0 / math.sqrt(row_total)
    weights = decoder_weight[0]
    features, width = weights.shape[1:]
    last = 2 * height
    first = row_total - last
    groups = (range(lines - 1), range(lines - 1, lines))
    hbm = pl.BlockSpec(memory_space=pltpu.HBM)
    struct = jax.ShapeDtypeStruct
    block_flops = 2 * row_total * features * width

    def swap_tok(value, step):
        return lax.ppermute(value, "tok", [(i, i ^ step) for i in range(ranks)])

    def swap_layer(value, step):
        return lax.ppermute(value, "layer", [(i, i ^ step) for i in range(layers)])

    def exchange(parts):
        arrived = list(parts)
        for step in reversed(range(1, layers)):
            arrived[step] = swap_layer(parts[step], step)
        return arrived

    def gather_lines(own, before=()):
        lane = {0: own}
        for line in sorted(range(1, lines), key=lambda j: (bin(j).count("1"), -j)):
            low = line & -line
            lane[line] = swap_tok(lane[line ^ low], 2 * low)
        here, *_ = lax.optimization_barrier((own, *before)) if before else (own,)
        main = [lane[j] for j in groups[0]]
        main += [swap_tok(lane[j] if j else here, 1) for j in groups[0]]
        return main, [lane[lines - 1]]

    def other_core(pieces, after):
        *pieces, _ = lax.optimization_barrier((*pieces, after))
        return pieces + [swap_tok(piece, 1) for piece in pieces]

    relative = []
    for group in groups:
        for core in range(2):
            relative += [2 * j + core for j in group]
    order = call(
        functools.partial(table_kernel, tuple(relative)),
        struct((row_total, row_total), BF16),
        whole(1),
        whole(1)[0],
        [pltpu.VMEM((row_total, row_total), F32)],
        6 * MICROSECOND,
        4 * row_total * row_total,
    )(row_order[None])

    main_inputs, last_inputs = gather_lines(layer_inputs[0], (order,))
    encode_operands = (encoder_weight[0], encoder_bias)
    main_own = call(
        functools.partial(encode_kernel, len(main_inputs)),
        struct((first, features), BF16),
        whole(len(main_inputs) + 2),
        whole(1)[0],
        [pltpu.VMEM((first, width), BF16)],
        2 * first * width * features,
        2 * width * features,
    )(*main_inputs[::-1], *encode_operands)
    main_acts = exchange([main_own] * layers)
    squares = call(
        norm_kernel,
        struct((layers, features), F32),
        whole(2),
        whole(1)[0],
        [],
        4 * layers * features * width,
        2 * layers * features * width,
    )(weights, main_own)
    last_inputs = other_core(last_inputs, squares)
    extra = -(-3 * layers // 16) * 16
    last_own = call(
        functools.partial(encode_last_kernel, len(last_inputs)),
        struct((last + extra, features), BF16),
        whole(len(last_inputs) + 3),
        whole(1)[0],
        [pltpu.VMEM((last, width), BF16), pltpu.VMEM((extra, features), F32)],
        2 * last * width * features,
        2 * width * features,
    )(*last_inputs, *encode_operands, squares)
    last_acts = exchange([last_own] * layers)
    first_sorted = call(
        functools.partial(sort_kernel, layers),
        struct((row_total, layers * features), F32),
        whole(layers + 1),
        whole(1)[0],
        [],
        2 * row_total * first * layers * features,
        2 * first * layers * features,
    )(order, *main_acts[::-1])

    columns = width
    acts_all, keep, send, far_keep, far_send, norms = call(
        functools.partial(decode_kernel, layers, last, columns),
        (
            struct((row_total, layers * features), BF16),
            *[struct((first // 2, width), BF16)] * 2,
            *[struct((last // 2, width), BF16)] * 2,
            struct((layers, features), F32),
        ),
        whole(3 + layers),
        tuple(whole(6)),
        [],
        layers * block_flops,
        2 * layers * features * width,
    )(order, first_sorted, *last_acts[::-1], weights)

    far = far_keep.astype(F32) + swap_tok(far_send, 1).astype(F32)
    near = keep.astype(F32) + swap_tok(send, 1).astype(F32)
    parts = [near[i * height : (i + 1) * height] for i in range(lines - 1)] + [far]
    blocks = {}
    for line in reversed(range(1, lines)):
        low = line & -line
        blocks[line] = parts[line].astype(BF16)
        if low == 1 and line + 1 in blocks:
            blocks[line], _ = lax.optimization_barrier((blocks[line], blocks[line + 1]))
        arrived = swap_tok(blocks[line], 2 * low)
        parts[line ^ low] = parts[line ^ low] + arrived.astype(F32)
    resid_full = (
        parts[0] + decoder_bias[0] - layer_targets[0].astype(F32)
    ) * loss_scale

    _, *late = lax.optimization_barrier((send, *main_inputs, *last_inputs))
    ordered, turned = call(
        functools.partial(order_kernel, len(late)),
        (struct((width, row_total), BF16), struct((layers, width, features), BF16)),
        whole(len(late) + 2),
        tuple(whole(2)),
        [pltpu.VMEM((row_total, width), BF16)],
        2 * row_total * row_total * width,
        4 * layers * features * width,
    )(*late, order, weights)
    resid_low, ordered, turned = lax.optimization_barrier(
        (resid_full.astype(BF16), ordered, turned)
    )
    main_resid, last_resid = gather_lines(resid_low)

    def grad_acts(pieces):
        count = len(pieces) * height
        *parts, rows = call(
            functools.partial(grad_kernel, layers, len(pieces)),
            (
                *[struct((count, features), BF16 if step else F32) for step in range(layers)],
                struct((count, width), BF16),
            ),
            whole(len(pieces) + 1),
            tuple(whole(layers + 1)),
            [],
            2 * count * layers * features * width,
            2 * layers * features * width,
        )(*pieces[::-1], turned)
        return parts[0], exchange(parts), rows

    main_grad, main_sums, main_rows = grad_acts(main_resid)
    last_resid = other_core(last_resid, main_grad)
    _, last_sums, last_rows = grad_acts(last_resid)

    tall = math.gcd(256, features)
    slots = min(8, layers * features // tall)
    decoder_grad, bias_grad = call(
        functools.partial(decoder_grad_kernel, loss_scale),
        (struct((layers, features, width), BF16), struct((1, width), F32)),
        whole(5),
        (hbm, whole(1)[0]),
        [
            pltpu.VMEM((row_total, width), BF16),
            pltpu.VMEM((slots, tall, width), BF16),
            pltpu.SemaphoreType.DMA((slots,)),
        ],
        layers * block_flops,
        4 * layers * features * width,
    )(acts_all, norms, main_rows, last_rows, weights)

    tall = min(512, width)
    encoder_grad, feature_grad = call(
        functools.partial(encoder_grad_kernel, layers, loss_scale, tall),
        (struct((width, features), BF16), struct((1, features), F32)),
        whole(3 + 2 * layers),
        (hbm, whole(1)[0]),
        [
            pltpu.VMEM((row_total, features), BF16),
            pltpu.VMEM((width, features), BF16),
            pltpu.SemaphoreType.DMA((width // tall,)),
        ],
        block_flops,
        2 * features * width,
    )(ordered, acts_all, norms, *main_sums[::-1], *last_sums[::-1])
    return (encoder_grad[None], feature_grad, decoder_grad[None], bias_grad)


def solution(mesh):
    placed = (
        P("layer", "tok", None),
        P("layer", "tok", None),
        P(),
        P("layer", None, "tok"),
        P("layer", "tok"),
        P("layer", None, "tok", None),
        P("layer", None),
    )
    return jax.shard_map(
        on_device,
        mesh=mesh,
        in_specs=placed,
        out_specs=(
            P("layer", None, "tok"),
            P("layer", "tok"),
            P("layer", None, "tok", None),
            P("layer", None),
        ),
        check_vma=False,
    )
```

```python
import functools
import math

import jax
import jax.numpy as jnp
from jax import lax
from jax.experimental import pallas as pl
from jax.experimental.pallas import tpu as pltpu
from jax.sharding import PartitionSpec as P

BF16 = jnp.bfloat16
F32 = jnp.float32
VMEM_LIMIT = 16 * 1024 * 1024
MICROSECOND = 1_150_000_000


def whole(count):
    return [pl.BlockSpec(memory_space=pltpu.VMEM)] * count


def call(kernel, out_shape, in_specs, out_specs, scratch, flops, moved, limit=VMEM_LIMIT):
    return pl.pallas_call(
        kernel,
        out_shape=out_shape,
        in_specs=in_specs,
        out_specs=out_specs,
        scratch_shapes=scratch,
        compiler_params=pltpu.CompilerParams(vmem_limit_bytes=limit),
        cost_estimate=pl.CostEstimate(flops=flops, bytes_accessed=moved, transcendentals=0),
    )


def table_kernel(relative, rows_ref, order, table):
    rank = lax.axis_index("tok")
    total_rows = table.shape[0]
    height = total_rows // len(relative)
    lane = lax.broadcasted_iota(jnp.int32, (1, total_rows), 1)
    held_rows = lane % height
    for index, offset in enumerate(relative):
        held_rows = held_rows + jnp.where(lane // height == index, (rank ^ offset) * height, 0)
    wanted = jnp.broadcast_to(rows_ref[...], (total_rows, total_rows)).T
    table[...] = jnp.where(wanted == held_rows, 1.0, 0.0)
    for index, offset in enumerate(relative):
        start = pl.multiple_of((rank ^ offset) * height, height)
        order[pl.ds(index * height, height), :] = table[pl.ds(start, height), :].astype(BF16)


def norm_kernel(weights, after, squares):
    layers, features, width = weights.shape
    target = lax.axis_index("layer")
    for source in range(layers):
        total = jnp.zeros((features, 128), F32)
        for part in range(width // 128):
            value = weights[source, :, pl.ds(part * 128, 128)].astype(F32)
            total = total + value * value
        column = jnp.sum(total, axis=1, keepdims=True)
        row = jnp.broadcast_to(column, (features, 128)).T[:1]
        squares[pl.ds(source, 1), :] = jnp.where(source <= target, row, 0.0)


def gather_rows(pieces, rows):
    height = pieces[0].shape[0]
    for index, piece in enumerate(pieces):
        rows[pl.ds(index * height, height), :] = piece[...]


def gather_parts(parts, rows):
    start = 0
    for part in parts:
        rows[pl.ds(start, part.shape[0]), :] = part[...]
        start += part.shape[0]


def encode_kernel(count, *refs):
    pieces, (weight, bias, out, rows) = refs[:count][::-1], refs[count:]
    gather_rows(pieces, rows)
    value = jnp.dot(rows[...], weight[...], preferred_element_type=F32) + bias[...]
    out[...] = jnp.maximum(value, 0.0).astype(BF16)


def encode_last_kernel(count, *refs):
    pieces, (weight, bias, squares, out, rows, extra) = refs[:count], refs[count:]
    gather_rows(pieces, rows)
    value = jnp.dot(rows[...], weight[...], preferred_element_type=F32) + bias[...]
    out[pl.ds(0, rows.shape[0]), :] = jnp.maximum(value, 0.0).astype(BF16)
    extra[...] = jnp.zeros(extra.shape, F32)
    rest = squares[...]
    layers = rest.shape[0]
    for part in range(3):
        term = rest.astype(BF16).astype(F32)
        extra[pl.ds(part * layers, layers), :] = term
        rest = rest - term
    out[pl.ds(rows.shape[0], extra.shape[0]), :] = extra[...].astype(BF16)


def sort_kernel(layers, order, *refs):
    acts, out = refs[:layers][::-1], refs[layers]
    target = lax.axis_index("layer")
    first, features = acts[0].shape
    for offset in range(layers):
        place = pl.ds(pl.multiple_of((target ^ offset) * features, features), features)
        out[:, place] = jnp.dot(order[:, :first], acts[offset][...], preferred_element_type=F32)


def decode_kernel(layers, last, columns, order_ref, first_sorted, *refs):
    acts, weights = refs[:layers][::-1], refs[layers]
    acts_out, keep, send, far_keep, far_send, norms = refs[layers + 1 :]
    target = lax.axis_index("layer")
    features, width = weights.shape[1:]
    total_rows = order_ref.shape[0]
    first = total_rows - last
    for offset in range(layers):
        source = target ^ offset
        place = pl.ds(pl.multiple_of(source * features, features), features)
        value = jnp.dot(
            order_ref[:, pl.ds(first, last)],
            acts[offset][pl.ds(0, last), :],
            preferred_element_type=F32,
        )
        used = jnp.where(source <= target, 1.0, 0.0)
        acts_out[:, place] = ((first_sorted[:, place] + value) * used).astype(BF16)
    near, far = first // 2, last // 2
    for part in range(width // columns):
        lanes = pl.ds(part * columns, columns)
        block = weights[:, :, lanes].reshape(layers * features, columns)
        value = jnp.dot(acts_out[...], block, preferred_element_type=F32).astype(BF16)
        keep[:, lanes] = value[:near]
        send[:, lanes] = value[near:first]
        far_keep[:, lanes] = value[first : first + far]
        far_send[:, lanes] = value[first + far :]
    total = jnp.zeros((layers, features), F32)
    for offset in range(layers):
        value = acts[offset][pl.ds(last, acts[0].shape[0] - last), :].astype(F32)
        for part in range(3):
            total = total + value[part * layers : (part + 1) * layers]
    norms[...] = jnp.sqrt(total + 1e-06)


def order_kernel(count, *refs):
    pieces, (order, weights, out, turned, rows) = refs[:count], refs[count:]
    gather_rows(pieces, rows)
    out[...] = lax.dot_general(
        rows[...], order[...], (((0,), (1,)), ((), ())), preferred_element_type=F32
    ).astype(BF16)
    for source in range(weights.shape[0]):
        turned[source] = weights[source].T


def grad_kernel(layers, count, *refs):
    pieces, turned = refs[:count][::-1], refs[count]
    outs, rows = refs[count + 1 : count + 1 + layers], refs[count + 1 + layers]
    target = lax.axis_index("layer")
    gather_rows(pieces, rows)
    for offset in range(layers):
        source = target ^ offset
        value = jnp.dot(rows[...], turned[source], preferred_element_type=F32)
        outs[offset][...] = jnp.where(source <= target, value, 0.0).astype(outs[offset].dtype)


def decoder_grad_kernel(loss_scale, acts, norms, main_rows, last_rows, weights, *refs):
    out, bias_out, rows, slots, sems = refs
    layers, features, width = weights.shape
    depth, tall = slots.shape[:2]
    steps = features // tall
    pending = [None] * depth
    gather_parts((main_rows, last_rows), rows)
    ones = jnp.ones((16, rows.shape[0]), BF16)
    bias_out[...] = jnp.dot(ones, rows[...], preferred_element_type=F32)[:1]
    for source in range(layers):
        used = source <= lax.axis_index("layer")
        for step in range(steps):
            slot = (source * steps + step) % depth
            if pending[slot] is not None:
                pending[slot].wait()
            block = acts[:, pl.ds(source * features + step * tall, tall)]
            sums = jnp.sum(block.astype(F32), axis=0, keepdims=True)
            norm = norms[pl.ds(source, 1), pl.ds(step * tall, tall)]
            factor_row = jnp.where(used, sums * loss_scale / norm, 0.0)
            factor = jnp.broadcast_to(factor_row, (128, tall)).T
            product = lax.dot_general(
                block, rows[...], (((0,), (0,)), ((), ())), preferred_element_type=F32
            )
            for part in range(width // 128):
                cut = slice(part * 128, part * 128 + 128)
                value = weights[source, pl.ds(step * tall, tall), cut].astype(F32)
                slots[slot, :, cut] = (product[:, cut] + factor * value).astype(BF16)
            copy = pltpu.make_async_copy(
                slots.at[slot], out.at[source, pl.ds(step * tall, tall)], sems.at[slot]
            )
            copy.start()
            pending[slot] = copy
    for copy in pending:
        if copy is not None:
            copy.wait()


def encoder_grad_kernel(layers, loss_scale, tall, ordered, acts, norms, *refs):
    main_parts, last_parts = refs[:layers][::-1], refs[layers : 2 * layers][::-1]
    out, sums_out, low, slots, sems = refs[2 * layers :]
    target = lax.axis_index("layer")
    features = main_parts[0].shape[1]
    place = pl.ds(pl.multiple_of(target * features, features), features)
    shift = norms[pl.ds(target, 1), :] * loss_scale
    sums = jnp.zeros((1, features), F32)
    start = 0
    for parts in (main_parts, last_parts):
        total = parts[0][...]
        rows = pl.ds(start, total.shape[0])
        start += total.shape[0]
        for part in parts[1:]:
            total = total + part[...].astype(F32)
        grad = jnp.where(acts[rows, place] > 0, total + shift, 0.0)
        sums = sums + jnp.sum(grad, axis=0, keepdims=True)
        low[rows, :] = grad.astype(BF16)
    sums_out[...] = sums
    width = ordered.shape[0]
    copies = []
    for step in range(width // tall):
        rows = pl.ds(step * tall, tall)
        slots[rows, :] = jnp.dot(
            ordered[rows, :], low[...], preferred_element_type=F32
        ).astype(BF16)
        copy = pltpu.make_async_copy(slots.at[rows], out.at[rows], sems.at[step])
        copy.start()
        copies.append(copy)
    for copy in copies:
        copy.wait()


def on_device(
    layer_inputs,
    layer_targets,
    row_order,
    encoder_weight,
    encoder_bias,
    decoder_weight,
    decoder_bias,
):
    layers = lax.axis_size("layer")
    ranks = lax.axis_size("tok")
    lines = ranks // 2
    row_total = row_order.shape[0]
    height = row_total // ranks
    loss_scale = 1.0 / math.sqrt(row_total)
    weights = decoder_weight[0]
    features, width = weights.shape[1:]
    last = 2 * height
    first = row_total - last
    groups = (range(lines - 1), range(lines - 1, lines))
    hbm = pl.BlockSpec(memory_space=pltpu.HBM)
    struct = jax.ShapeDtypeStruct
    block_flops = 2 * row_total * features * width

    def swap_tok(value, step):
        return lax.ppermute(value, "tok", [(i, i ^ step) for i in range(ranks)])

    def swap_layer(value, step):
        return lax.ppermute(value, "layer", [(i, i ^ step) for i in range(layers)])

    def exchange(parts):
        arrived = list(parts)
        for step in reversed(range(1, layers)):
            arrived[step] = swap_layer(parts[step], step)
        return arrived

    def gather_lines(own, before=()):
        lane = {0: own}
        for line in sorted(range(1, lines), key=lambda j: (bin(j).count("1"), -j)):
            low = line & -line
            lane[line] = swap_tok(lane[line ^ low], 2 * low)
        here, *_ = lax.optimization_barrier((own, *before)) if before else (own,)
        main = [lane[j] for j in groups[0]]
        main += [swap_tok(lane[j] if j else here, 1) for j in groups[0]]
        return main, [lane[lines - 1]]

    def other_core(pieces, after):
        *pieces, _ = lax.optimization_barrier((*pieces, after))
        return pieces + [swap_tok(piece, 1) for piece in pieces]

    relative = []
    for group in groups:
        for core in range(2):
            relative += [2 * j + core for j in group]
    order = call(
        functools.partial(table_kernel, tuple(relative)),
        struct((row_total, row_total), BF16),
        whole(1),
        whole(1)[0],
        [pltpu.VMEM((row_total, row_total), F32)],
        6 * MICROSECOND,
        4 * row_total * row_total,
    )(row_order[None])

    main_inputs, last_inputs = gather_lines(layer_inputs[0], (order,))
    encode_operands = (encoder_weight[0], encoder_bias)
    main_own = call(
        functools.partial(encode_kernel, len(main_inputs)),
        struct((first, features), BF16),
        whole(len(main_inputs) + 2),
        whole(1)[0],
        [pltpu.VMEM((first, width), BF16)],
        2 * first * width * features,
        2 * width * features,
    )(*main_inputs[::-1], *encode_operands)
    main_acts = exchange([main_own] * layers)
    squares = call(
        norm_kernel,
        struct((layers, features), F32),
        whole(2),
        whole(1)[0],
        [],
        4 * layers * features * width,
        2 * layers * features * width,
    )(weights, main_own)
    last_inputs = other_core(last_inputs, squares)
    extra = -(-3 * layers // 16) * 16
    last_own = call(
        functools.partial(encode_last_kernel, len(last_inputs)),
        struct((last + extra, features), BF16),
        whole(len(last_inputs) + 3),
        whole(1)[0],
        [pltpu.VMEM((last, width), BF16), pltpu.VMEM((extra, features), F32)],
        2 * last * width * features,
        2 * width * features,
    )(*last_inputs, *encode_operands, squares)
    last_acts = exchange([last_own] * layers)
    first_sorted = call(
        functools.partial(sort_kernel, layers),
        struct((row_total, layers * features), F32),
        whole(layers + 1),
        whole(1)[0],
        [],
        2 * row_total * first * layers * features,
        2 * first * layers * features,
    )(order, *main_acts[::-1])

    columns = width
    acts_all, keep, send, far_keep, far_send, norms = call(
        functools.partial(decode_kernel, layers, last, columns),
        (
            struct((row_total, layers * features), BF16),
            *[struct((first // 2, width), BF16)] * 2,
            *[struct((last // 2, width), BF16)] * 2,
            struct((layers, features), F32),
        ),
        whole(3 + layers),
        tuple(whole(6)),
        [],
        layers * block_flops,
        2 * layers * features * width,
    )(order, first_sorted, *last_acts[::-1], weights)

    far = far_keep.astype(F32) + swap_tok(far_send, 1).astype(F32)
    near = keep.astype(F32) + swap_tok(send, 1).astype(F32)
    parts = [near[i * height : (i + 1) * height] for i in range(lines - 1)] + [far]
    blocks = {}
    for line in reversed(range(1, lines)):
        low = line & -line
        blocks[line] = parts[line].astype(BF16)
        arrived = swap_tok(blocks[line], 2 * low)
        parts[line ^ low] = parts[line ^ low] + arrived.astype(F32)
    resid_full = (
        parts[0] + decoder_bias[0] - layer_targets[0].astype(F32)
    ) * loss_scale

    _, *late = lax.optimization_barrier((send, *main_inputs, *last_inputs))
    ordered, turned = call(
        functools.partial(order_kernel, len(late)),
        (struct((width, row_total), BF16), struct((layers, width, features), BF16)),
        whole(len(late) + 2),
        tuple(whole(2)),
        [pltpu.VMEM((row_total, width), BF16)],
        2 * row_total * row_total * width,
        4 * layers * features * width,
    )(*late, order, weights)
    resid_low, ordered, turned = lax.optimization_barrier(
        (resid_full.astype(BF16), ordered, turned)
    )
    main_resid, last_resid = gather_lines(resid_low)

    def grad_acts(pieces):
        count = len(pieces) * height
        *parts, rows = call(
            functools.partial(grad_kernel, layers, len(pieces)),
            (
                *[struct((count, features), BF16 if step else F32) for step in range(layers)],
                struct((count, width), BF16),
            ),
            whole(len(pieces) + 1),
            tuple(whole(layers + 1)),
            [],
            2 * count * layers * features * width,
            2 * layers * features * width,
        )(*pieces[::-1], turned)
        return parts[0], exchange(parts), rows

    main_grad, main_sums, main_rows = grad_acts(main_resid)
    last_resid = other_core(last_resid, main_grad)
    _, last_sums, last_rows = grad_acts(last_resid)

    tall = math.gcd(256, features)
    slots = min(8, layers * features // tall)
    decoder_grad, bias_grad = call(
        functools.partial(decoder_grad_kernel, loss_scale),
        (struct((layers, features, width), BF16), struct((1, width), F32)),
        whole(5),
        (hbm, whole(1)[0]),
        [
            pltpu.VMEM((row_total, width), BF16),
            pltpu.VMEM((slots, tall, width), BF16),
            pltpu.SemaphoreType.DMA((slots,)),
        ],
        layers * block_flops,
        4 * layers * features * width,
    )(acts_all, norms, main_rows, last_rows, weights)

    tall = min(512, width)
    encoder_grad, feature_grad = call(
        functools.partial(encoder_grad_kernel, layers, loss_scale, tall),
        (struct((width, features), BF16), struct((1, features), F32)),
        whole(3 + 2 * layers),
        (hbm, whole(1)[0]),
        [
            pltpu.VMEM((row_total, features), BF16),
            pltpu.VMEM((width, features), BF16),
            pltpu.SemaphoreType.DMA((width // tall,)),
        ],
        block_flops,
        2 * features * width,
    )(ordered, acts_all, norms, *main_sums[::-1], *last_sums[::-1])
    return (encoder_grad[None], feature_grad, decoder_grad[None], bias_grad)


def solution(mesh):
    placed = (
        P("layer", "tok", None),
        P("layer", "tok", None),
        P(),
        P("layer", None, "tok"),
        P("layer", "tok"),
        P("layer", None, "tok", None),
        P("layer", None),
    )
    return jax.shard_map(
        on_device,
        mesh=mesh,
        in_specs=placed,
        out_specs=(
            P("layer", None, "tok"),
            P("layer", "tok"),
            P("layer", None, "tok", None),
            P("layer", None),
        ),
        check_vma=False,
    )
```
